512 devices in a mesh: sp: 64 (over z, x), dp: 8 (over y, core).
Axes of the slice: x: 4, y: 4, z: 16, core: 2. Of those that a mesh axis runs over, the one named last changes fastest.
Arguments:
- hidden_in: bfloat16 [49152, 1024], P(('dp', 'sp')), parts along dimension 0, may hold values from -6 to 6
- queries: bfloat16 [49152, 2048], P(('dp', 'sp')), parts along dimension 0, may hold values from -6 to 6
- keys: bfloat16 [49152, 256], P(('dp', 'sp')), parts along dimension 0, may hold values from -6 to 6
- values: bfloat16 [49152, 256], P(('dp', 'sp')), parts along dimension 0, may hold values from -6 to 6
- q_gain: float32 [128], replicated, may hold values from 0.5 to 1.5
- k_gain: float32 [128], replicated, may hold values from 0.5 to 1.5
- out_weight: bfloat16 [2048, 1024], P(None, 'sp'), may hold values from -0.125 to 0.125
- moe_gain: float32 [1024], replicated, may hold values from 0.5 to 1.5
- expert_ids: int32 [49152, 8], P(('dp', 'sp')), parts along dimension 0, may hold values from 0 to 63, all different within a row; in each aligned block of 96 rows (0 to 95, 96 to 191, ...) at most 15 rows name the same one
- route_weights: float32 [49152, 8], P(('dp', 'sp')), parts along dimension 0, may hold values from 0.05 to 1
- gate_proj: bfloat16 [64, 1024, 384], P('sp'), may hold values from -0.1875 to 0.1875
- up_proj: bfloat16 [64, 1024, 384], P('sp'), may hold values from -0.1875 to 0.1875
- down_proj: bfloat16 [64, 384, 1024], P('sp'), may hold values from -0.3125 to 0.3125
Outputs:
- layer_out: bfloat16 [49152, 1024], P(('dp', 'sp')), parts along dimension 0
The draws below stay inside these ranges and needn't reach their ends.
There are 8 independent parts, one for each index of `dp`. The reference program is written for one: setup_inputs(seed, part) draws one part's arguments, and reference() takes and returns one part's arrays. A program takes and returns all parts, laid end to end along the dimension named above; an argument that names none is the same for every part. Nothing has to cross between parts.
Inputs may be any that keep to these rules, and one draw needn't show every extreme that they name: `expert_ids`: each row names 8 different experts. Among the rows of one index of sp no expert is named more than 15 times; some expert is named exactly 15 times.
All inputs are finite; a program needn't handle non-finite values.
Results may differ from the reference program's by a relative error of at most 0.0075.
Values may be sent and summed in bfloat16 or wider, within the bound.
A program may use at most 128 MiB of HBM per device.

```python
import math
import jax
import jax.numpy as jnp
import numpy as np
from jax import lax

D = 1024
HQW = 16
HKW = 2
HD = 128
FW = 384
TOP = 8
TOK_DEV = 96
SEQ = 6144
EXPERTS = 64
CAP = 15


def steps_of(own_key, dims, cuts, low, top_value):
    factor_of, own = 1.0, jax.random.fold_in(own_key, 6)
    for dim, parts in cuts:
        draws = jnp.exp(jax.random.uniform(jax.random.fold_in(own, dim), (parts,), jnp.float32, low / len(cuts), top_value / len(cuts)))
        factor_of = factor_of * jnp.repeat(draws, dims[dim] // parts).reshape([-1 if axis == dim else 1 for axis in range(len(dims))])
    return factor_of


def assign_block(key, own, number, rows, count, top, most, skew):
    ranking = jax.random.permutation(key, count)
    packed, ordinary = shares(count, rows * top, most, skew, True), shares(count, rows * top, most, skew, False)
    places = jnp.arange(count)

    def named(tallies, offset_by):
        used = int((tallies > 0).sum())
        fixed = max(1, used // 4)
        moved = fixed + (places - fixed + offset_by * (used - fixed)) % max(1, count - fixed)
        return jnp.zeros((count,), jnp.int32).at[ranking[jnp.where(places < fixed, places, moved)]].set(jnp.asarray(tallies, jnp.int32))

    tallies = jnp.where(number % 4 == 0, named(packed, number // 4), named(ordinary, number - number // 4 - 1))
    mixed = jax.random.permutation(jax.random.fold_in(own, 3), count)
    source_of, receiver = mixed[0:count // 2 * 2:2], mixed[1:count // 2 * 2:2]
    margin = jnp.minimum(tallies[source_of] - 1, most - tallies[receiver]) // 2
    margin = jnp.where((source_of == ranking[0]) | (receiver == ranking[0]) | (tallies[receiver] == 0), 0, jnp.maximum(margin, 0))
    moved = jax.random.randint(jax.random.fold_in(own, 4), (count // 2,), 0, 1 << 20) % (margin + 1)
    tallies = tallies.at[source_of].add(-moved).at[receiver].add(moved)
    labels = jnp.searchsorted(jnp.cumsum(tallies), jnp.arange(rows * top), side="right").astype(jnp.int32)
    grid = labels.reshape(top, rows).T
    grid = grid[jax.random.permutation(jax.random.fold_in(own, 1), rows)]
    offset_by = jax.random.randint(jax.random.fold_in(own, 2), (rows, 1), 0, top)
    return jnp.take_along_axis(grid, (jnp.arange(top)[None, :] + offset_by) % top, axis=1)


def shares(count, total, most, slope, full):
    weights = [(1 << 20) // math.isqrt(grade ** slope) + 1 for grade in range(1, count + 1)]
    largest = most if full else min(most, max(-(-total // count), total * weights[0] // sum(weights)))
    least = 1 if total - largest >= count - 1 else 0
    holding, surplus = [largest] + [least] * (count - 1), total - largest - least * (count - 1)
    while surplus > 0:
        movable = [i for i in range(1, count) if holding[i] < largest] or [i for i in range(1, count) if holding[i] < most]
        pool, budget = sum([weights[i] for i in movable]), surplus
        for i in movable:
            more = min(most - holding[i], max(1, budget * weights[i] // pool), surplus)
            holding[i] = holding[i] + more
            surplus = surplus - more
    return np.array(holding)


def bell_draw(rng, extent, spread, bound, shards=(), kind=jnp.bfloat16):
    entries = jax.random.normal(rng, extent, jnp.float32) * spread
    if len(shards) > 0:
        entries = steps_of(rng, extent, shards, -0.22, 0.18) * entries
    return jnp.clip(entries, min=-bound, max=bound).astype(kind)


def setup_inputs(seed: int = 0, part: int = 0) -> dict:
    streams_of = jax.random.split(jax.random.key(seed), 14)
    part_splits = jax.random.split(jax.random.fold_in(streams_of[13], part), 14)
    hidden_in = bell_draw(part_splits[0], (SEQ, D), 1.0, 6.0, ((0, 64),))
    queries = bell_draw(part_splits[1], (SEQ, HQW * HD), 1.0, 6.0, ((0, 64),))
    keys = bell_draw(part_splits[2], (SEQ, HKW * HD), 1.0, 6.0, ((0, 64),))
    values = bell_draw(part_splits[3], (SEQ, HKW * HD), 1.0, 6.0, ((0, 64),))
    q_gain = jnp.clip(1.0 + 0.1 * jax.random.normal(streams_of[4], (HD,), jnp.float32), 0.5, 1.5)
    k_gain = jnp.clip(1.0 + 0.1 * jax.random.normal(streams_of[5], (HD,), jnp.float32), 0.5, 1.5)
    out_weight = bell_draw(streams_of[6], (HQW * HD, D), (HQW * HD) ** -0.5, 0.125, ((1, 64),))
    moe_gain = jnp.clip(1.0 + 0.1 * jax.random.normal(streams_of[7], (D,), jnp.float32), 0.5, 1.5)
    expert_ids_keys = jax.random.split(jax.random.fold_in(part_splits[8], 1), SEQ // TOK_DEV)
    expert_ids_turns = jax.random.permutation(jax.random.fold_in(part_splits[8], 3), SEQ // TOK_DEV)
    expert_ids = jax.vmap(lambda own, number: assign_block(jax.random.fold_in(part_splits[8], 2), own, number, TOK_DEV, EXPERTS, TOP, CAP, 2))(expert_ids_keys, expert_ids_turns).reshape((SEQ, TOP))
    route_weights = jnp.clip(jnp.exp(math.log(1.0) - 2.9957323 * jax.random.uniform(part_splits[9], (SEQ, TOP), jnp.float32) ** steps_of(part_splits[9], (SEQ, TOP), ((0, 64),), -0.2, 0.2)), 0.05, 1.0)
    gate_proj = bell_draw(streams_of[10], (EXPERTS, D, FW), D ** -0.5, 0.1875, ((0, 64),))
    up_proj = bell_draw(streams_of[11], (EXPERTS, D, FW), D ** -0.5, 0.1875, ((0, 64),))
    down_proj = bell_draw(streams_of[12], (EXPERTS, FW, D), FW ** -0.5, 0.3125, ((0, 64),))
    return dict(hidden_in=hidden_in, queries=queries, keys=keys, values=values, q_gain=q_gain, k_gain=k_gain, out_weight=out_weight, moe_gain=moe_gain, expert_ids=expert_ids, route_weights=route_weights, gate_proj=gate_proj, up_proj=up_proj, down_proj=down_proj)


EPS = 1e-06
THETA = 1000000.0

def head_norm(values_in, gain):
    meansq = lax.optimization_barrier(jnp.mean(values_in * values_in, axis=-1, keepdims=True))
    return values_in * lax.rsqrt(meansq + EPS) * gain

def rotate(values_in, positions):
    half = values_in.shape[-1] // 2
    expo = jnp.arange(half).astype(jnp.float32) * (-2.0 / values_in.shape[-1])
    freq = jnp.power(jnp.float32(THETA), expo)
    angle = positions.astype(jnp.float32)[:, None] * freq[None, :]
    cosv = jnp.cos(angle)[:, None, :]
    sinv = jnp.sin(angle)[:, None, :]
    first = values_in[..., :half]
    second = values_in[..., half:]
    return jnp.concatenate([first * cosv - second * sinv, second * cosv + first * sinv], axis=-1)

def reference(hidden_in, queries, keys, values, q_gain, k_gain, out_weight, moe_gain, expert_ids, route_weights, gate_proj, up_proj, down_proj):
    seq = hidden_in.shape[0]
    positions = jnp.arange(seq).astype(jnp.int32)
    group = HQW // HKW
    q_rot = rotate(head_norm(queries.astype(jnp.float32).reshape(seq, HQW, HD), q_gain.astype(jnp.float32)), positions).astype(jnp.bfloat16)
    k_rot = rotate(head_norm(keys.astype(jnp.float32).reshape(seq, HKW, HD), k_gain.astype(jnp.float32)), positions).astype(jnp.bfloat16)
    q_heads = jnp.transpose(q_rot, (1, 0, 2))
    k_heads = jnp.repeat(jnp.transpose(k_rot, (1, 0, 2)), group, axis=0)
    v_heads = jnp.repeat(jnp.transpose(values.reshape(seq, HKW, HD), (1, 0, 2)), group, axis=0)
    causal = positions[:, None] >= positions[None, :]
    scale = 1.0 / math.sqrt(HD)

    def one_head(operands):
        q_one, k_one, v_one = operands
        scores = jnp.dot(q_one, k_one.T, preferred_element_type=jnp.float32) * scale
        expw = jnp.where(causal, jnp.exp(scores), 0.0)
        numer = jnp.dot(expw.astype(jnp.bfloat16), v_one, preferred_element_type=jnp.float32)
        return numer / lax.optimization_barrier(jnp.sum(expw, axis=-1))[:, None]
    heads_out = lax.map(one_head, (q_heads, k_heads, v_heads))
    context = jnp.transpose(heads_out, (1, 0, 2)).reshape(seq, HQW * HD).astype(jnp.bfloat16)
    attn_out = jnp.dot(context, out_weight, preferred_element_type=jnp.float32).astype(jnp.bfloat16)
    resid = hidden_in.astype(jnp.float32) + attn_out.astype(jnp.float32)
    meansq = lax.optimization_barrier(jnp.mean(resid * resid, axis=-1, keepdims=True))
    normed = (resid * lax.rsqrt(meansq + EPS) * moe_gain.astype(jnp.float32)).astype(jnp.bfloat16)
    coef = route_weights / lax.optimization_barrier(jnp.sum(route_weights, axis=-1, keepdims=True))
    chosen = (expert_ids[:, :, None] == jnp.arange(EXPERTS).astype(jnp.int32)[None, None, :]).astype(jnp.float32)
    combine = lax.optimization_barrier(jnp.sum(chosen * coef[:, :, None], axis=1))

    def one_expert(total, operands):
        w_gate, w_up, w_down, weight_col = operands
        gate = jnp.dot(normed, w_gate, preferred_element_type=jnp.float32)
        upv = jnp.dot(normed, w_up, preferred_element_type=jnp.float32)
        mid = (jax.nn.silu(gate) * upv).astype(jnp.bfloat16)
        result = jnp.dot(mid, w_down, preferred_element_type=jnp.float32).astype(jnp.bfloat16)
        return (total + weight_col[:, None] * result.astype(jnp.float32), None)
    total, unused = lax.scan(one_expert, jnp.zeros((seq, D), jnp.float32), (gate_proj, up_proj, down_proj, combine.T))
    return (resid + total).astype(jnp.bfloat16)
```

```python
import functools
import math

import jax
import jax.numpy as jnp
from jax import lax
from jax.experimental import pallas as pl
from jax.experimental.pallas import tpu as pltpu
from jax.sharding import PartitionSpec as P

EPS = 1e-06
THETA = 1000000.0
MESH = pl.DeviceIdType.MESH
F32 = jnp.float32
BF16 = jnp.bfloat16

TOK = 96
ZN = 16
SLOT = 16
PIECES = ((64, 16), (64, 16), (32, 12))
NPIECE = 44
FIRST, PER_STEP, PER_HOP = 6, 2, 3
NT = (((1,), (1,)), ((), ()))


def dot(a, b):
    return jnp.dot(a, b, preferred_element_type=F32)


def dot_nt(a, b):
    return lax.dot_general(a, b, NT, preferred_element_type=F32)


def copy_to(src, dst, send, recv, sp, dp):
    return pltpu.make_async_remote_copy(
        src_ref=src, dst_ref=dst, send_sem=send, recv_sem=recv,
        device_id={"sp": sp, "dp": dp}, device_id_type=MESH,
    )


def place():
    sp = lax.axis_index("sp")
    g = lax.axis_index("dp")
    z = sp // 4
    x = sp % 4
    return z, x, g, g // 2, g % 2


def signal(sem, sp, dp):
    pl.semaphore_signal(sem, inc=1, device_id={"sp": sp, "dp": dp}, device_id_type=MESH)


def route_kernel(ids_ref, idst_ref, rw_ref, d_ref, c_ref):
    slots = 64 * SLOT
    top = ids_ref.shape[1]

    def order(e):
        return (e & 31) * 2 + (e >> 5)

    ids = order(ids_ref[...])
    idst = order(idst_ref[...])
    rw = rw_ref[...]
    coef = rw / jnp.sum(rw, axis=-1, keepdims=True)
    mt = jnp.zeros((64, TOK), F32)
    m = jnp.zeros((TOK, 64), F32)
    cm = jnp.zeros((TOK, 64), F32)
    e0 = lax.broadcasted_iota(jnp.int32, (64, TOK), 0)
    e1 = lax.broadcasted_iota(jnp.int32, (TOK, 64), 1)
    for k in range(top):
        mt = mt + jnp.where(idst[k : k + 1, :] == e0, 1.0, 0.0)
        hit = ids[:, k : k + 1] == e1
        m = m + jnp.where(hit, 1.0, 0.0)
        cm = cm + jnp.where(hit, coef[:, k : k + 1], 0.0)
    r = lax.broadcasted_iota(jnp.int32, (TOK, TOK), 0)
    q = lax.broadcasted_iota(jnp.int32, (TOK, TOK), 1)
    upper = jnp.where(r < q, 1.0, 0.0).astype(BF16)
    lower = jnp.where(q < r, 1.0, 0.0).astype(BF16)
    mtb = mt.astype(BF16)
    mb = m.astype(BF16)
    post = dot(mtb, upper).astype(BF16)
    pos = dot(lower, mb).astype(BF16)
    s0 = lax.broadcasted_iota(jnp.int32, (slots, 64), 0)
    x1 = lax.broadcasted_iota(jnp.int32, (slots, 64), 1)
    rep = jnp.where((s0 >> 4) == x1, 1.0, 0.0).astype(BF16)
    x0 = lax.broadcasted_iota(jnp.int32, (64, slots), 0)
    s1 = lax.broadcasted_iota(jnp.int32, (64, slots), 1)
    rept = jnp.where((s1 >> 4) == x0, 1.0, 0.0).astype(BF16)
    lane = (lax.broadcasted_iota(jnp.int32, (slots, TOK), 0) & 15).astype(F32)
    d_ref[...] = jnp.where(dot(rep, mtb) > 0.5, jnp.where(dot(rep, post) == lane, 1.0, 0.0), 0.0).astype(BF16)
    lanet = (lax.broadcasted_iota(jnp.int32, (TOK, slots), 1) & 15).astype(F32)
    keep = jnp.where(dot(mb, rept) > 0.5, jnp.where(dot(pos, rept) == lanet, 1.0, 0.0), 0.0)
    hi = cm.astype(BF16)
    lo = (cm - hi.astype(F32)).astype(BF16)
    c_ref[0:TOK, :] = (dot(hi, rept) * keep).astype(BF16)
    c_ref[TOK : 2 * TOK, :] = (dot(lo, rept) * keep).astype(BF16)


def layer_kernel(
    q_ref, k_ref, v_ref, qg_ref, kg_ref, cos_ref, sin_ref, wt_ref,
    hid_ref, gain_ref, d_ref, c_ref, gate_ref, up_ref, down_ref,
    out_ref,
    qsend, kvsend, qbuf, qall, kvbuf, acc, den, ctx, wz, wfull, pstage, pbuf,
    resid, outb, inb, yb, retb, wg, wu, wd,
    q_s, q_r, kv_s, kv_r, up_s, up_r, dn_s, dn_r, sib_s, sib_r, wz_s, wz_r, wf_s, wf_r, p_s, p_r,
    own_sem, wup_s, wup_r, wdn_s, wdn_r, loc, a_s, a_r, b_s, b_r,
):
    z, x, g, y, c = place()
    sp = z * 4 + x
    q_idx = g * 4 + x
    up_sp = ((z + 1) % ZN) * 4 + x
    dn_sp = ((z + ZN - 1) % ZN) * 4 + x
    sib = y * 2 + (1 - c)
    is_self = c == x // 2
    own_k = z // 8
    source = z % 8 == g
    inner = jnp.logical_not(source)
    p_ring = (z - g + ZN) % ZN

    barrier = pltpu.get_barrier_semaphore()

    def loop(lo, hi, fn):
        def one(i, carry):
            fn(i)
            return carry

        lax.fori_loop(lo, hi, one, 0)

    loop(1, ZN, lambda o: signal(barrier, ((z + o) % ZN) * 4 + x, g))

    def slice_peer(o):
        t = (q_idx + o) % 32
        return t, z * 4 + t % 4, t // 4

    def greet(o):
        t, psp, pdp = slice_peer(o)
        signal(barrier, psp, pdp)

    loop(1, 32, greet)

    stores = (wg, wu, wd)
    own = [
        pltpu.make_async_copy(src, dst.at[own_k], own_sem.at[i])
        for i, (src, dst) in enumerate(zip((gate_ref, up_ref, down_ref), stores))
    ]

    @pl.when(source)
    def _():
        for copy in own:
            copy.start()

    cosv = cos_ref[...]
    sinv = sin_ref[...]

    def turned(val, gain):
        val = val.astype(F32)
        ms = jnp.mean(val * val, axis=-1, keepdims=True)
        n = val * lax.rsqrt(ms + EPS) * gain
        return (n * cosv + pltpu.roll(n, 64, 1) * sinv).astype(BF16)

    for h in range(2):
        kvsend[h, :, 0:128] = turned(k_ref[:, h * 128 : (h + 1) * 128], kg_ref[...])
        kvsend[h, :, 128:256] = v_ref[:, h * 128 : (h + 1) * 128]
    for h in range(2):
        for n in range(8):
            at = (h * 8 + n) * 128
            qsend[h, :, n * 128 : (n + 1) * 128] = turned(q_ref[:, at : at + 128], qg_ref[...])

    pl.semaphore_wait(barrier, 46)

    rows = pl.ds(pl.multiple_of((x % 2) * TOK, TOK), TOK)
    dest_dp = y * 2 + x // 2
    for h in range(2):
        dest_sp = z * 4 + 2 * c + h
        here = jnp.logical_and(is_self, x % 2 == h)
        kv_dst = kvbuf.at[z, x // 2, rows, :]
        q_dst = qbuf.at[x % 2]

        @pl.when(here)
        def _():
            pltpu.make_async_copy(kvsend.at[h], kv_dst, kv_r.at[x % 2]).start()
            pltpu.make_async_copy(qsend.at[h], q_dst, q_r.at[x % 2]).start()

        @pl.when(jnp.logical_not(here))
        def _():
            copy_to(kvsend.at[h], kv_dst, kv_s.at[h], kv_r.at[x % 2], dest_sp, dest_dp).start()
            copy_to(qsend.at[h], q_dst, q_s.at[h], q_r.at[x % 2], dest_sp, dest_dp).start()

    def wz_copy(o):
        return copy_to(wt_ref, wz.at[own_k], wz_s.at[o], wz_r.at[own_k], ((z + o) % ZN) * 4 + x, g)

    @pl.when(source)
    def _():
        wz[own_k] = wt_ref[...]
        loop(1, ZN, lambda o: wz_copy(o).start())

    k_up = p_ring // 8
    k_dn = jnp.where(source, k_up, 1 - k_up)
    k_up_in = ((p_ring + ZN - 1) % ZN) // 8
    far_up = p_ring % 8
    far_dn = (ZN - p_ring) % 8
    down = far_dn != 7

    def piece(j, fn):
        at = 0
        for store, (n_rows, count) in zip(stores, PIECES):
            first = at

            @pl.when(jnp.logical_and(j >= first, j < first + count))
            def _():
                start = pl.multiple_of((j - first) * n_rows, n_rows)
                fn(lambda k: store.at[k, pl.ds(start, n_rows), :])

            at += count

    def wup(ref, j):
        return copy_to(ref, ref, wup_s.at[j], wup_r.at[j], up_sp, g)

    def wdn(ref, j):
        return copy_to(ref, ref, wdn_s.at[j], wdn_r.at[j], dn_sp, g)

    def one_up(j):
        def act(ref):
            @pl.when(inner)
            def _():
                wup(ref(k_up_in), j).wait_recv()

            wup(ref(k_up), j).start()

        piece(j, act)

    def one_dn(j):
        def act(ref):
            @pl.when(inner)
            def _():
                wdn(ref(k_dn), j).wait_recv()

            @pl.when(down)
            def _():
                wdn(ref(k_dn), j).start()

        piece(j, act)

    def reach(t, far):
        return jnp.clip(FIRST + PER_STEP * t - PER_HOP * far, 0, NPIECE)

    def ring(t):
        for far, act in ((far_up, one_up), (far_dn, one_dn)):
            lo = jnp.where(jnp.logical_and(t == 0, inner), 0, reach(t, far))
            loop(lo, reach(t + 1, far), act)

    @pl.when(source)
    def _():
        for copy in own:
            copy.wait()
        loop(0, FIRST, one_up)
        loop(0, FIRST, one_dn)


    for t in range(2):
        kdst = kvbuf.at[z, c, pl.ds(t * TOK, TOK), :]
        pltpu.make_async_copy(kdst, kdst, kv_r.at[t]).wait()

    def up_copy(s, slice_idx):
        ref = kvbuf.at[slice_idx, c]
        return copy_to(ref, ref, up_s.at[s], up_r.at[s], up_sp, g)

    def dn_copy(s, slice_idx):
        ref = kvbuf.at[slice_idx, c]
        return copy_to(ref, ref, dn_s.at[s], dn_r.at[s], dn_sp, g)

    def sib_copy(i, slice_idx, half):
        ref = kvbuf.at[slice_idx, half]
        return copy_to(ref, ref, sib_s.at[i], sib_r.at[i], sp, sib)

    up_copy(1, z).start()
    dn_copy(1, z).start()
    sib_copy(0, z, c).start()

    for t in range(2):
        pltpu.make_async_copy(qbuf.at[t], qbuf.at[t], q_r.at[t]).wait()
    for n in range(8):
        for t in range(2):
            qall[n * 192 + t * TOK : n * 192 + (t + 1) * TOK, :] = qbuf[t, :, n * 128 : (n + 1) * 128]

    factor = math.log2(math.e) / math.sqrt(128)

    def attend(slice_idx, diagonal):
        kv = kvbuf[slice_idx]
        kk = kv[:, :, 0:128].reshape(384, 128)
        vv = kv[:, :, 128:256].reshape(384, 128)
        for n in range(4):
            at = slice(n * 384, (n + 1) * 384)
            s = dot_nt(qall[at, :], kk)
            p = jnp.exp2(s * factor)
            if diagonal:
                r = lax.broadcasted_iota(jnp.int32, (384, 384), 0)
                r = jnp.where(r >= 192, r - 192, r) + c * 192
                col = lax.broadcasted_iota(jnp.int32, (384, 384), 1)
                p = jnp.where(col <= r, p, 0.0)
            part = p[:, 0:128] + p[:, 128:256] + p[:, 256:384]
            pv = dot(p.astype(BF16), vv)
            if diagonal:
                den[at, :] = part
                acc[at, :] = pv
            else:
                den[at, :] = den[at, :] + part
                acc[at, :] = acc[at, :] + pv

    sib_copy(0, z, 1 - c).wait_recv()
    attend(z, True)

    def step(s):
        below = (z - s + ZN) % ZN
        above = (z + s) % ZN
        up_copy(s, below).wait_recv()

        @pl.when(s < 8)
        def _():
            up_copy(s + 1, below).start()

        sib_copy(2 * s, below, c).start()

        @pl.when(s < 8)
        def _():
            dn_copy(s, above).wait_recv()

            @pl.when(s < 7)
            def _():
                dn_copy(s + 1, above).start()

            sib_copy(2 * s + 1, above, c).start()

        ring(s - 1)
        sib_copy(2 * s, below, 1 - c).wait_recv()

        @pl.when(z >= s)
        def _():
            attend(below, False)

        @pl.when(s < 8)
        def _():
            sib_copy(2 * s + 1, above, 1 - c).wait_recv()

            @pl.when(z + s >= ZN)
            def _():
                attend(above, False)

    loop(1, 5, step)

    for k in range(2):

        @pl.when(jnp.logical_not(jnp.logical_and(source, own_k == k)))
        def _():
            pltpu.make_async_copy(wz.at[k], wz.at[k], wz_r.at[k]).wait()

    def wf_copy(o):
        t, psp, pdp = slice_peer(o)
        cols = pl.ds(pl.multiple_of((t % 2) * 1024, 1024), 1024)
        return copy_to(wz.at[:, :, cols], wfull.at[:, q_idx], wf_s.at[o], wf_r.at[o], psp, pdp)

    loop(1, 32, lambda o: wf_copy(o).start())
    mine = pl.ds(pl.multiple_of((x % 2) * 1024, 1024), 1024)
    local = pltpu.make_async_copy(wz.at[:, :, mine], wfull.at[:, q_idx], loc.at[0])
    local.start()

    loop(5, 9, step)

    for n in range(8):
        at = slice(n * 192, (n + 1) * 192)
        total = jnp.sum(den[at, :], axis=-1, keepdims=True)
        ctx[:, n * 128 : (n + 1) * 128] = (acc[at, :] / total).astype(BF16)
    local.wait()
    loop(1, 32, lambda o: wf_copy(o).wait_recv())
    for b in range(4):
        w = wfull[b // 2, (b % 2) * 16 : (b % 2 + 1) * 16].reshape(256, 1024)
        part = dot_nt(ctx[...], w).astype(BF16)
        for t in range(2):
            pstage[t, :, b * 256 : (b + 1) * 256] = part[t * TOK : (t + 1) * TOK, :]
    for t in range(2):
        here = jnp.logical_and(is_self, x % 2 == t)
        dst = pbuf.at[x % 2]

        @pl.when(here)
        def _():
            pltpu.make_async_copy(pstage.at[t], dst, p_r.at[x % 2]).start()

        @pl.when(jnp.logical_not(here))
        def _():
            copy_to(pstage.at[t], dst, p_s.at[t], p_r.at[x % 2], z * 4 + 2 * c + t, dest_dp).start()

    ring(8)
    ring(9)
    for h in range(2):
        pltpu.make_async_copy(pbuf.at[h], pbuf.at[h], p_r.at[h]).wait()

    attn = (pbuf[0].astype(F32) + pbuf[1].astype(F32)).astype(BF16).astype(F32)
    res = hid_ref[...].astype(F32) + attn
    resid[...] = res
    ms = jnp.mean(res * res, axis=-1, keepdims=True)
    normed = (res * lax.rsqrt(ms + EPS) * gain_ref[...]).astype(BF16)

    def there(o):
        t, psp, pdp = slice_peer(o)
        return copy_to(outb.at[t], inb.at[:, q_idx], a_s.at[o], a_r.at[o], psp, pdp)

    def back(o):
        t, psp, pdp = slice_peer(o)
        return copy_to(yb.at[:, t], retb.at[q_idx], b_s.at[o], b_r.at[o], psp, pdp)

    for b in range(4):
        part = dot(d_ref[b * 256 : (b + 1) * 256, :], normed).astype(BF16)
        outb[b * 8 : (b + 1) * 8] = part.reshape(8, 2, SLOT, 1024)
    loop(1, 32, lambda o: there(o).start())
    keep = pltpu.make_async_copy(outb.at[q_idx], inb.at[:, q_idx], loc.at[1])
    keep.start()

    def rest(i):
        for far, act in ((far_up, one_up), (far_dn, one_dn)):
            j = i - PER_HOP * far

            @pl.when(jnp.logical_and(j >= 0, j < NPIECE))
            def _():
                act(j)

    loop(FIRST + PER_STEP * 10, NPIECE + PER_HOP * 7, rest)

    @pl.when(source)
    def _():
        loop(0, NPIECE, lambda j: piece(j, lambda ref: wup(ref(k_up_in), j).wait_recv()))

    keep.wait()
    loop(1, 32, lambda o: there(o).wait_recv())
    for k in range(2):
        tokens = inb[k].reshape(512, 1024)
        gate = dot(tokens, wg[k])
        upv = dot(tokens, wu[k])
        mid = (gate / (1.0 + jnp.exp(-gate)) * upv).astype(BF16)
        yb[k] = dot(mid, wd[k]).astype(BF16).reshape(32, SLOT, 1024)
    loop(1, 32, lambda o: back(o).start())
    keep2 = pltpu.make_async_copy(yb.at[:, q_idx], retb.at[q_idx], loc.at[2])
    keep2.start()

    @pl.when(source)
    def _():
        loop(1, ZN, lambda o: wz_copy(o).wait_send())

    loop(0, NPIECE, lambda j: piece(j, lambda ref: wup(ref(k_up), j).wait_send()))

    @pl.when(down)
    def _():
        loop(0, NPIECE, lambda j: piece(j, lambda ref: wdn(ref(k_dn), j).wait_send()))

    loop(1, 32, lambda o: wf_copy(o).wait_send())
    loop(1, 9, lambda s: up_copy(s, z).wait_send())
    loop(1, 8, lambda s: dn_copy(s, z).wait_send())
    sib_copy(0, z, c).wait_send()
    loop(2, 17, lambda i: sib_copy(i, z, c).wait_send())
    for h in range(2):
        here = jnp.logical_and(is_self, x % 2 == h)

        @pl.when(jnp.logical_not(here))
        def _():
            dst = kvbuf.at[z, x // 2, rows, :]
            dest_sp = z * 4 + 2 * c + h
            copy_to(kvsend.at[h], dst, kv_s.at[h], kv_r.at[x % 2], dest_sp, dest_dp).wait_send()
            copy_to(qsend.at[h], qbuf.at[x % 2], q_s.at[h], q_r.at[x % 2], dest_sp, dest_dp).wait_send()
            copy_to(pstage.at[h], pbuf.at[x % 2], p_s.at[h], p_r.at[x % 2], dest_sp, dest_dp).wait_send()

    loop(1, 32, lambda o: there(o).wait_send())
    keep2.wait()
    loop(1, 32, lambda o: back(o).wait_recv())
    mixed = dot(c_ref[...], retb[...].reshape(1024, 1024))
    out_ref[...] = (resid[...] + (mixed[0:TOK, :] + mixed[TOK : 2 * TOK, :])).astype(BF16)
    loop(1, 32, lambda o: back(o).wait_send())


def body(
    hidden_in, queries, keys, values, q_gain, k_gain, out_weight, moe_gain,
    expert_ids, route_weights, gate_proj, up_proj, down_proj,
):
    sp = lax.axis_index("sp")
    positions = sp * TOK + jnp.arange(TOK, dtype=jnp.int32)
    expo = jnp.arange(64).astype(F32) * (-2.0 / 128)
    freq = jnp.power(jnp.float32(THETA), expo)
    angle = positions.astype(F32)[:, None] * freq[None, :]
    cosv = jnp.cos(angle)
    sinv = jnp.sin(angle)
    cos2 = jnp.concatenate([cosv, cosv], axis=-1)
    sin2 = jnp.concatenate([-sinv, sinv], axis=-1)
    vm = pl.BlockSpec(memory_space=pltpu.VMEM)
    hbm = pl.BlockSpec(memory_space=pl.ANY)
    dma = pltpu.SemaphoreType.DMA

    disp, comb = pl.pallas_call(
        route_kernel,
        out_shape=(jax.ShapeDtypeStruct((1024, TOK), BF16), jax.ShapeDtypeStruct((2 * TOK, 1024), BF16)),
        in_specs=[vm] * 3,
        out_specs=(vm, vm),
        name="route",
    )(expert_ids, expert_ids.T, route_weights)

    return pl.pallas_call(
        layer_kernel,
        out_shape=jax.ShapeDtypeStruct((TOK, 1024), BF16),
        in_specs=[vm] * 12 + [hbm] * 3,
        out_specs=vm,
        scratch_shapes=[
            pltpu.VMEM((2, TOK, 1024), BF16),
            pltpu.VMEM((2, TOK, 256), BF16),
            pltpu.VMEM((2, TOK, 1024), BF16),
            pltpu.VMEM((1536, 128), BF16),
            pltpu.VMEM((ZN, 2, 192, 256), BF16),
            pltpu.VMEM((1536, 128), F32),
            pltpu.VMEM((1536, 128), F32),
            pltpu.VMEM((192, 1024), BF16),
            pltpu.VMEM((2, 16, 2048), BF16),
            pltpu.VMEM((2, 32, 16, 1024), BF16),
            pltpu.VMEM((2, TOK, 1024), BF16),
            pltpu.VMEM((2, TOK, 1024), BF16),
            pltpu.VMEM((TOK, 1024), F32),
            pltpu.VMEM((32, 2, SLOT, 1024), BF16),
            pltpu.VMEM((2, 32, SLOT, 1024), BF16),
            pltpu.VMEM((2, 32, SLOT, 1024), BF16),
            pltpu.VMEM((32, 2, SLOT, 1024), BF16),
            pltpu.VMEM((2, 1024, 384), BF16),
            pltpu.VMEM((2, 1024, 384), BF16),
            pltpu.VMEM((2, 384, 1024), BF16),
            dma((2,)), dma((2,)), dma((2,)), dma((2,)),
            dma((9,)), dma((9,)), dma((9,)), dma((9,)),
            dma((17,)), dma((17,)),
            dma((16,)), dma((2,)), dma((32,)), dma((32,)),
            dma((2,)), dma((2,)), dma((3,)),
            dma((NPIECE,)), dma((NPIECE,)), dma((NPIECE,)), dma((NPIECE,)),
            dma((3,)),
            dma((32,)), dma((32,)), dma((32,)), dma((32,)),
        ],
        compiler_params=pltpu.CompilerParams(
            collective_id=0, has_side_effects=True, vmem_limit_bytes=48 * 1024 * 1024
        ),
        name="layer",
    )(
        queries, keys, values, q_gain.reshape(1, 128), k_gain.reshape(1, 128), cos2, sin2, out_weight.T,
        hidden_in, moe_gain.reshape(1, 1024), disp, comb, gate_proj[0], up_proj[0], down_proj[0],
    )


def solution(mesh):
    tok = P(("dp", "sp"), None)
    return jax.shard_map(
        body,
        mesh=mesh,
        in_specs=(
            tok, tok, tok, tok, P(), P(), P(None, "sp"), P(), tok, tok,
            P("sp", None, None), P("sp", None, None), P("sp", None, None),
        ),
        out_specs=tok,
        check_vma=False,
    )
```

```python
import functools
import math

import jax
import jax.numpy as jnp
from jax import lax
from jax.experimental import pallas as pl
from jax.experimental.pallas import tpu as pltpu
from jax.sharding import PartitionSpec as P

EPS = 1e-06
THETA = 1000000.0
MESH = pl.DeviceIdType.MESH
F32 = jnp.float32
BF16 = jnp.bfloat16

TOK = 96
ZN = 16
SLOT = 16
PIECES = ((64, 16), (64, 16), (32, 12))
NPIECE = 44
FIRST, PER_STEP, PER_HOP = 6, 2, 3
NT = (((1,), (1,)), ((), ()))


def dot(a, b):
    return jnp.dot(a, b, preferred_element_type=F32)


def dot_nt(a, b):
    return lax.dot_general(a, b, NT, preferred_element_type=F32)


def copy_to(src, dst, send, recv, sp, dp):
    return pltpu.make_async_remote_copy(
        src_ref=src, dst_ref=dst, send_sem=send, recv_sem=recv,
        device_id={"sp": sp, "dp": dp}, device_id_type=MESH,
    )


def place():
    sp = lax.axis_index("sp")
    g = lax.axis_index("dp")
    z = sp // 4
    x = sp % 4
    return z, x, g, g // 2, g % 2


def signal(sem, sp, dp):
    pl.semaphore_signal(sem, inc=1, device_id={"sp": sp, "dp": dp}, device_id_type=MESH)


def route(idst, rwt, d_ref, c_ref):
    slots = 64 * SLOT
    order = (idst & 31) * 2 + (idst >> 5)
    coef = rwt / jnp.sum(rwt, axis=0, keepdims=True)
    hits = jnp.zeros((64, TOK), F32)
    weights = jnp.zeros((64, TOK), F32)
    expert = lax.broadcasted_iota(jnp.int32, (64, TOK), 0)
    for k in range(idst.shape[0]):
        hit = order[k : k + 1, :] == expert
        hits = hits + jnp.where(hit, 1.0, 0.0)
        weights = weights + jnp.where(hit, coef[k : k + 1, :], 0.0)
    r = lax.broadcasted_iota(jnp.int32, (TOK, TOK), 0)
    q = lax.broadcasted_iota(jnp.int32, (TOK, TOK), 1)
    earlier = jnp.where(r < q, 1.0, 0.0).astype(BF16)
    hits = hits.astype(BF16)
    before = dot(hits, earlier).astype(BF16)
    hi = weights.astype(BF16)
    lo = (weights - hi.astype(F32)).astype(BF16)
    for b in range(slots // 256):
        s0 = lax.broadcasted_iota(jnp.int32, (256, 64), 0) + b * 256
        e1 = lax.broadcasted_iota(jnp.int32, (256, 64), 1)
        rep = jnp.where((s0 >> 4) == e1, 1.0, 0.0).astype(BF16)
        lane = (lax.broadcasted_iota(jnp.int32, (256, TOK), 0) & 15).astype(F32)
        keep = jnp.where(dot(rep, hits) > 0.5, jnp.where(dot(rep, before) == lane, 1.0, 0.0), 0.0)
        at = slice(b * 256, (b + 1) * 256)
        d_ref[at, :] = keep.astype(BF16)
        c_ref[0:TOK, at] = jnp.transpose(dot(rep, hi) * keep).astype(BF16)
        c_ref[TOK : 2 * TOK, at] = jnp.transpose(dot(rep, lo) * keep).astype(BF16)


def layer_kernel(
    q_hbm, k_hbm, v_hbm, qg_hbm, kg_hbm, cos_hbm, sin_hbm, wt_hbm,
    hid_hbm, gain_hbm, idst_hbm, rwt_hbm, gate_ref, up_ref, down_ref,
    out_ref,
    q_ref, k_ref, v_ref, qg_ref, kg_ref, cos_ref, sin_ref, wt_ref,
    hid_ref, gain_ref, idst_ref, rwt_ref, d_ref, c_ref, in_sem,
    qsend, kvsend, qbuf, qall, kvbuf, acc, den, ctx, wz, wfull, pstage, pbuf,
    resid, outb, inb, yb, retb, wg, wu, wd,
    q_s, q_r, kv_s, kv_r, up_s, up_r, dn_s, dn_r, sib_s, sib_r, wz_s, wz_r, wf_s, wf_r, p_s, p_r,
    own_sem, wup_s, wup_r, wdn_s, wdn_r, loc, a_s, a_r, b_s, b_r,
):
    z, x, g, y, c = place()
    sp = z * 4 + x
    q_idx = g * 4 + x
    up_sp = ((z + 1) % ZN) * 4 + x
    dn_sp = ((z + ZN - 1) % ZN) * 4 + x
    sib = y * 2 + (1 - c)
    is_self = c == x // 2
    own_k = z // 8
    source = z % 8 == g
    inner = jnp.logical_not(source)
    p_ring = (z - g + ZN) % ZN

    pairs = (
        (q_hbm, q_ref), (k_hbm, k_ref), (v_hbm, v_ref), (qg_hbm, qg_ref), (kg_hbm, kg_ref), (cos_hbm, cos_ref),
        (sin_hbm, sin_ref), (wt_hbm, wt_ref), (hid_hbm, hid_ref), (gain_hbm, gain_ref), (idst_hbm, idst_ref),
        (rwt_hbm, rwt_ref),
    )
    loads = [pltpu.make_async_copy(src, dst, in_sem.at[i]) for i, (src, dst) in enumerate(pairs)]
    for load in loads:
        load.start()
    barrier = pltpu.get_barrier_semaphore()

    def loop(lo, hi, fn):
        def one(i, carry):
            fn(i)
            return carry

        lax.fori_loop(lo, hi, one, 0)

    loop(1, ZN, lambda o: signal(barrier, ((z + o) % ZN) * 4 + x, g))

    def slice_peer(o):
        t = (q_idx + o) % 32
        return t, z * 4 + t % 4, t // 4

    def greet(o):
        t, psp, pdp = slice_peer(o)
        signal(barrier, psp, pdp)

    loop(1, 32, greet)

    stores = (wg, wu, wd)
    own = [
        pltpu.make_async_copy(src, dst.at[own_k], own_sem.at[i])
        for i, (src, dst) in enumerate(zip((gate_ref, up_ref, down_ref), stores))
    ]

    @pl.when(source)
    def _():
        for copy in own:
            copy.start()

    for i in (1, 2, 4, 5, 6):
        loads[i].wait()
    cosv = cos_ref[...]
    sinv = sin_ref[...]

    def turned(val, gain):
        val = val.astype(F32)
        ms = jnp.mean(val * val, axis=-1, keepdims=True)
        n = val * lax.rsqrt(ms + EPS) * gain
        return (n * cosv + pltpu.roll(n, 64, 1) * sinv).astype(BF16)

    for h in range(2):
        kvsend[h, :, 0:128] = turned(k_ref[:, h * 128 : (h + 1) * 128], kg_ref[...])
        kvsend[h, :, 128:256] = v_ref[:, h * 128 : (h + 1) * 128]
    pl.semaphore_wait(barrier, 46)

    rows = pl.ds(pl.multiple_of((x % 2) * TOK, TOK), TOK)
    dest_dp = y * 2 + x // 2

    def to_chip(h, src, dst, send, recv):
        here = jnp.logical_and(is_self, x % 2 == h)

        @pl.when(here)
        def _():
            pltpu.make_async_copy(src, dst, recv).start()

        @pl.when(jnp.logical_not(here))
        def _():
            copy_to(src, dst, send, recv, z * 4 + 2 * c + h, dest_dp).start()

    for h in range(2):
        to_chip(h, kvsend.at[h], kvbuf.at[z, x // 2, rows, :], kv_s.at[h], kv_r.at[x % 2])
    for i in (0, 3, 7, 8, 9, 10, 11):
        loads[i].wait()
    for h in range(2):
        for n in range(8):
            at = (h * 8 + n) * 128
            qsend[h, :, n * 128 : (n + 1) * 128] = turned(q_ref[:, at : at + 128], qg_ref[...])
        to_chip(h, qsend.at[h], qbuf.at[x % 2], q_s.at[h], q_r.at[x % 2])

    def wz_copy(o):
        return copy_to(wt_ref, wz.at[own_k], wz_s.at[o], wz_r.at[own_k], ((z + o) % ZN) * 4 + x, g)

    @pl.when(source)
    def _():
        wz[own_k] = wt_ref[...]
        loop(1, ZN, lambda o: wz_copy(o).start())

    k_up = p_ring // 8
    k_dn = jnp.where(source, k_up, 1 - k_up)
    k_up_in = ((p_ring + ZN - 1) % ZN) // 8
    far_up = p_ring % 8
    far_dn = (ZN - p_ring) % 8
    down = far_dn != 7

    def piece(j, fn):
        at = 0
        for store, (n_rows, count) in zip(stores, PIECES):
            first = at

            @pl.when(jnp.logical_and(j >= first, j < first + count))
            def _():
                start = pl.multiple_of((j - first) * n_rows, n_rows)
                fn(lambda k: store.at[k, pl.ds(start, n_rows), :])

            at += count

    def wup(ref, j):
        return copy_to(ref, ref, wup_s.at[j], wup_r.at[j], up_sp, g)

    def wdn(ref, j):
        return copy_to(ref, ref, wdn_s.at[j], wdn_r.at[j], dn_sp, g)

    def one_up(j):
        def act(ref):
            @pl.when(inner)
            def _():
                wup(ref(k_up_in), j).wait_recv()

            wup(ref(k_up), j).start()

        piece(j, act)

    def one_dn(j):
        def act(ref):
            @pl.when(inner)
            def _():
                wdn(ref(k_dn), j).wait_recv()

            @pl.when(down)
            def _():
                wdn(ref(k_dn), j).start()

        piece(j, act)

    def reach(t, far):
        return jnp.clip(FIRST + PER_STEP * t - PER_HOP * far, 0, NPIECE)

    def ring(t):
        for far, act in ((far_up, one_up), (far_dn, one_dn)):
            lo = jnp.where(jnp.logical_and(t == 0, inner), 0, reach(t, far))
            loop(lo, reach(t + 1, far), act)

    @pl.when(source)
    def _():
        for copy in own:
            copy.wait()
        loop(0, FIRST, one_up)
        loop(0, FIRST, one_dn)


    route(idst_ref[...], rwt_ref[...], d_ref, c_ref)

    for t in range(2):
        kdst = kvbuf.at[z, c, pl.ds(t * TOK, TOK), :]
        pltpu.make_async_copy(kdst, kdst, kv_r.at[t]).wait()

    def up_copy(s, slice_idx):
        ref = kvbuf.at[slice_idx, c]
        return copy_to(ref, ref, up_s.at[s], up_r.at[s], up_sp, g)

    def dn_copy(s, slice_idx):
        ref = kvbuf.at[slice_idx, c]
        return copy_to(ref, ref, dn_s.at[s], dn_r.at[s], dn_sp, g)

    def sib_copy(i, slice_idx, half):
        ref = kvbuf.at[slice_idx, half]
        return copy_to(ref, ref, sib_s.at[i], sib_r.at[i], sp, sib)

    @pl.when(z < ZN - 1)
    def _():
        up_copy(1, z).start()

    @pl.when(z <= 6)
    def _():
        dn_copy(1, z).start()

    sib_copy(0, z, c).start()

    for t in range(2):
        pltpu.make_async_copy(qbuf.at[t], qbuf.at[t], q_r.at[t]).wait()
    for n in range(8):
        for t in range(2):
            qall[n * 192 + t * TOK : n * 192 + (t + 1) * TOK, :] = qbuf[t, :, n * 128 : (n + 1) * 128]

    factor = math.log2(math.e) / math.sqrt(128)

    def attend(slice_idx, diagonal):
        kv = kvbuf[slice_idx]
        kk = kv[:, :, 0:128].reshape(384, 128)
        vv = kv[:, :, 128:256].reshape(384, 128)
        for n in range(4):
            at = slice(n * 384, (n + 1) * 384)
            s = dot_nt(qall[at, :], kk)
            p = jnp.exp2(s * factor)
            if diagonal:
                r = lax.broadcasted_iota(jnp.int32, (384, 384), 0)
                r = jnp.where(r >= 192, r - 192, r) + c * 192
                col = lax.broadcasted_iota(jnp.int32, (384, 384), 1)
                p = jnp.where(col <= r, p, 0.0)
            part = p[:, 0:128] + p[:, 128:256] + p[:, 256:384]
            pv = dot(p.astype(BF16), vv)
            if diagonal:
                den[at, :] = part
                acc[at, :] = pv
            else:
                den[at, :] = den[at, :] + part
                acc[at, :] = acc[at, :] + pv

    for k in range(2):

        @pl.when(jnp.logical_not(jnp.logical_and(source, own_k == k)))
        def _():
            pltpu.make_async_copy(wz.at[k], wz.at[k], wz_r.at[k]).wait()

    def wf_copy(o):
        t = (y * 4 + x + o) % 16
        cols = pl.ds(pl.multiple_of((t % 2) * 1024, 1024), 1024)
        return copy_to(
            wz.at[:, :, cols], wfull.at[:, y, c, x], wf_s.at[o], wf_r.at[o], z * 4 + t % 4, (t // 4) * 2 + c
        )

    def wf_sib(half):
        ref = wfull.at[:, :, half]
        return copy_to(ref, ref, wf_s.at[0], wf_r.at[0], sp, sib)

    loop(1, 16, lambda o: wf_copy(o).start())
    mine = pl.ds(pl.multiple_of((x % 2) * 1024, 1024), 1024)
    local = pltpu.make_async_copy(wz.at[:, :, mine], wfull.at[:, y, c, x], loc.at[0])
    local.start()

    sib_copy(0, z, 1 - c).wait_recv()
    attend(z, True)

    def step(s):
        below = (z - s + ZN) % ZN
        above = (z + s) % ZN
        from_below = z >= s
        above_on = jnp.logical_and(s < 8, jnp.logical_or(z + s <= 6, z + s >= ZN))
        above_used = jnp.logical_and(s < 8, z + s >= ZN)

        @pl.when(from_below)
        def _():
            up_copy(s, below).wait_recv()

            @pl.when(jnp.logical_and(s < 8, z < ZN - 1))
            def _():
                up_copy(s + 1, below).start()

            sib_copy(2 * s, below, c).start()

        @pl.when(above_on)
        def _():
            dn_copy(s, above).wait_recv()

            @pl.when(s < 7)
            def _():
                dn_copy(s + 1, above).start()

        @pl.when(above_used)
        def _():
            sib_copy(2 * s + 1, above, c).start()

        ring(s - 1)

        @pl.when(from_below)
        def _():
            sib_copy(2 * s, below, 1 - c).wait_recv()
            attend(below, False)

        @pl.when(above_used)
        def _():
            sib_copy(2 * s + 1, above, 1 - c).wait_recv()
            attend(above, False)

    loop(1, 6, step)
    loop(1, 16, lambda o: wf_copy(o).wait_recv())
    local.wait()
    wf_sib(c).start()
    loop(6, 9, step)

    for n in range(8):
        at = slice(n * 192, (n + 1) * 192)
        total = jnp.sum(den[at, :], axis=-1, keepdims=True)
        ctx[:, n * 128 : (n + 1) * 128] = (acc[at, :] / total).astype(BF16)
    wf_sib(1 - c).wait_recv()
    for b in range(4):
        w = wfull[b // 2, (b % 2) * 2 : (b % 2 + 1) * 2].reshape(256, 1024)
        part = dot_nt(ctx[...], w).astype(BF16)
        for t in range(2):
            pstage[t, :, b * 256 : (b + 1) * 256] = part[t * TOK : (t + 1) * TOK, :]
    for t in range(2):
        to_chip(t, pstage.at[t], pbuf.at[x % 2], p_s.at[t], p_r.at[x % 2])

    ring(8)
    ring(9)
    for h in range(2):
        pltpu.make_async_copy(pbuf.at[h], pbuf.at[h], p_r.at[h]).wait()

    attn = (pbuf[0].astype(F32) + pbuf[1].astype(F32)).astype(BF16).astype(F32)
    res = hid_ref[...].astype(F32) + attn
    resid[...] = res
    ms = jnp.mean(res * res, axis=-1, keepdims=True)
    normed = (res * lax.rsqrt(ms + EPS) * gain_ref[...]).astype(BF16)

    def first_of(dp):
        return (((z - dp + ZN) % ZN + 3) // 8) % 2

    def there(o, r):
        t, psp, pdp = slice_peer(o)
        kk = (first_of(pdp) + r) % 2
        return copy_to(outb.at[t, kk], inb.at[kk, q_idx], a_s.at[r, o], a_r.at[r, o], psp, pdp)

    def back(o, r):
        t, psp, pdp = slice_peer(o)
        kk = (first_of(g) + r) % 2
        return copy_to(yb.at[kk, t], retb.at[q_idx, kk], b_s.at[r, o], b_r.at[r, o], psp, pdp)

    def run_expert(r):
        kk = (first_of(g) + r) % 2
        loop(1, 32, lambda o: there(o, r).wait_recv())
        tokens = inb[kk].reshape(512, 1024)
        gate = dot(tokens, wg[kk])
        upv = dot(tokens, wu[kk])
        mid = (gate / (1.0 + jnp.exp(-gate)) * upv).astype(BF16)
        yb[kk] = dot(mid, wd[kk]).astype(BF16).reshape(32, SLOT, 1024)
        loop(1, 32, lambda o: back(o, r).start())
        keep = pltpu.make_async_copy(yb.at[kk, q_idx], retb.at[q_idx, kk], loc.at[2 + r])
        keep.start()
        return keep

    for b in range(4):
        part = dot(d_ref[b * 256 : (b + 1) * 256, :], normed).astype(BF16)
        outb[b * 8 : (b + 1) * 8] = part.reshape(8, 2, SLOT, 1024)
    loop(1, 32, lambda o: there(o, 0).start())
    loop(1, 32, lambda o: there(o, 1).start())
    keep = pltpu.make_async_copy(outb.at[q_idx], inb.at[:, q_idx], loc.at[1])
    keep.start()

    def rest(i):
        for far, act in ((far_up, one_up), (far_dn, one_dn)):
            j = i - PER_HOP * far

            @pl.when(jnp.logical_and(j >= 0, j < NPIECE))
            def _():
                act(j)

    loop(FIRST + PER_STEP * 10, NPIECE + PER_HOP * 4, rest)
    keep.wait()
    keep_first = run_expert(0)
    loop(NPIECE + PER_HOP * 4, NPIECE + PER_HOP * 7, rest)

    @pl.when(source)
    def _():
        loop(0, NPIECE, lambda j: piece(j, lambda ref: wup(ref(k_up_in), j).wait_recv()))

    keep_second = run_expert(1)

    @pl.when(source)
    def _():
        loop(1, ZN, lambda o: wz_copy(o).wait_send())

    loop(0, NPIECE, lambda j: piece(j, lambda ref: wup(ref(k_up), j).wait_send()))

    @pl.when(down)
    def _():
        loop(0, NPIECE, lambda j: piece(j, lambda ref: wdn(ref(k_dn), j).wait_send()))

    loop(1, 16, lambda o: wf_copy(o).wait_send())
    wf_sib(c).wait_send()

    def kv_sent(s):
        @pl.when(jnp.logical_and(z >= s - 1, z < ZN - 1))
        def _():
            up_copy(s, z).wait_send()

        @pl.when(jnp.logical_and(s < 8, jnp.logical_or(z + s <= 7, z + s >= ZN + 1)))
        def _():
            dn_copy(s, z).wait_send()

        @pl.when(z >= s)
        def _():
            sib_copy(2 * s, z, c).wait_send()

        @pl.when(jnp.logical_and(s < 8, z + s >= ZN))
        def _():
            sib_copy(2 * s + 1, z, c).wait_send()

    sib_copy(0, z, c).wait_send()
    loop(1, 9, kv_sent)
    for h in range(2):
        here = jnp.logical_and(is_self, x % 2 == h)

        @pl.when(jnp.logical_not(here))
        def _():
            dst = kvbuf.at[z, x // 2, rows, :]
            dest_sp = z * 4 + 2 * c + h
            copy_to(kvsend.at[h], dst, kv_s.at[h], kv_r.at[x % 2], dest_sp, dest_dp).wait_send()
            copy_to(qsend.at[h], qbuf.at[x % 2], q_s.at[h], q_r.at[x % 2], dest_sp, dest_dp).wait_send()
            copy_to(pstage.at[h], pbuf.at[x % 2], p_s.at[h], p_r.at[x % 2], dest_sp, dest_dp).wait_send()

    for r in range(2):
        loop(1, 32, lambda o, r=r: there(o, r).wait_send())
    keep_first.wait()
    keep_second.wait()
    for r in range(2):
        loop(1, 32, lambda o, r=r: back(o, r).wait_recv())
    mixed = dot(c_ref[...], retb[...].reshape(1024, 1024))
    out_ref[...] = (resid[...] + (mixed[0:TOK, :] + mixed[TOK : 2 * TOK, :])).astype(BF16)
    for r in range(2):
        loop(1, 32, lambda o, r=r: back(o, r).wait_send())


def body(
    hidden_in, queries, keys, values, q_gain, k_gain, out_weight, moe_gain,
    expert_ids, route_weights, gate_proj, up_proj, down_proj,
):
    sp = lax.axis_index("sp")
    positions = sp * TOK + jnp.arange(TOK, dtype=jnp.int32)
    expo = jnp.arange(64).astype(F32) * (-2.0 / 128)
    freq = jnp.power(jnp.float32(THETA), expo)
    angle = positions.astype(F32)[:, None] * freq[None, :]
    cosv = jnp.cos(angle)
    sinv = jnp.sin(angle)
    cos2 = jnp.concatenate([cosv, cosv], axis=-1)
    sin2 = jnp.concatenate([-sinv, sinv], axis=-1)
    vm = pl.BlockSpec(memory_space=pltpu.VMEM)
    hbm = pl.BlockSpec(memory_space=pltpu.HBM)
    dma = pltpu.SemaphoreType.DMA

    return pl.pallas_call(
        layer_kernel,
        out_shape=jax.ShapeDtypeStruct((TOK, 1024), BF16),
        in_specs=[hbm] * 15,
        out_specs=vm,
        scratch_shapes=[
            pltpu.VMEM((TOK, 2048), BF16),
            pltpu.VMEM((TOK, 256), BF16),
            pltpu.VMEM((TOK, 256), BF16),
            pltpu.VMEM((1, 128), F32),
            pltpu.VMEM((1, 128), F32),
            pltpu.VMEM((TOK, 128), F32),
            pltpu.VMEM((TOK, 128), F32),
            pltpu.VMEM((16, 2048), BF16),
            pltpu.VMEM((TOK, 1024), BF16),
            pltpu.VMEM((1, 1024), F32),
            pltpu.VMEM((8, TOK), jnp.int32),
            pltpu.VMEM((8, TOK), F32),
            pltpu.VMEM((64 * SLOT, TOK), BF16),
            pltpu.VMEM((2 * TOK, 64 * SLOT), BF16),
            dma((12,)),
            pltpu.VMEM((2, TOK, 1024), BF16),
            pltpu.VMEM((2, TOK, 256), BF16),
            pltpu.VMEM((2, TOK, 1024), BF16),
            pltpu.VMEM((1536, 128), BF16),
            pltpu.VMEM((ZN, 2, 192, 256), BF16),
            pltpu.VMEM((1536, 128), F32),
            pltpu.VMEM((1536, 128), F32),
            pltpu.VMEM((192, 1024), BF16),
            pltpu.VMEM((2, 16, 2048), BF16),
            pltpu.VMEM((2, 4, 2, 4, 16, 1024), BF16),
            pltpu.VMEM((2, TOK, 1024), BF16),
            pltpu.VMEM((2, TOK, 1024), BF16),
            pltpu.VMEM((TOK, 1024), F32),
            pltpu.VMEM((32, 2, SLOT, 1024), BF16),
            pltpu.VMEM((2, 32, SLOT, 1024), BF16),
            pltpu.VMEM((2, 32, SLOT, 1024), BF16),
            pltpu.VMEM((32, 2, SLOT, 1024), BF16),
            pltpu.VMEM((2, 1024, 384), BF16),
            pltpu.VMEM((2, 1024, 384), BF16),
            pltpu.VMEM((2, 384, 1024), BF16),
            dma((2,)), dma((2,)), dma((2,)), dma((2,)),
            dma((9,)), dma((9,)), dma((9,)), dma((9,)),
            dma((17,)), dma((17,)),
            dma((16,)), dma((2,)), dma((16,)), dma((16,)),
            dma((2,)), dma((2,)), dma((4,)),
            dma((NPIECE,)), dma((NPIECE,)), dma((NPIECE,)), dma((NPIECE,)),
            dma((4,)),
            dma((2, 32)), dma((2, 32)), dma((2, 32)), dma((2, 32)),
        ],
        compiler_params=pltpu.CompilerParams(
            collective_id=0, has_side_effects=True, vmem_limit_bytes=63 * 1024 * 1024
        ),
        name="layer",
    )(
        queries, keys, values, q_gain.reshape(1, 128), k_gain.reshape(1, 128), cos2, sin2, out_weight.T,
        hidden_in, moe_gain.reshape(1, 1024), expert_ids.T, route_weights.T, gate_proj[0], up_proj[0], down_proj[0],
    )


def solution(mesh):
    tok = P(("dp", "sp"), None)
    return jax.shard_map(
        body,
        mesh=mesh,
        in_specs=(
            tok, tok, tok, tok, P(), P(), P(None, "sp"), P(), tok, tok,
            P("sp", None, None), P("sp", None, None), P("sp", None, None),
        ),
        out_specs=tok,
        check_vma=False,
    )
```

```python
import functools
import math

import jax
import jax.numpy as jnp
from jax import lax
from jax.experimental import pallas as pl
from jax.experimental.pallas import tpu as pltpu
from jax.sharding import PartitionSpec as P

EPS = 1e-06
THETA = 1000000.0
MESH = pl.DeviceIdType.MESH
F32 = jnp.float32
BF16 = jnp.bfloat16

TOK = 96
ZN = 16
SLOT = 16
PIECES = ((64, 16), (64, 16), (32, 12))
NPIECE = 44
FIRST, PER_STEP, LAG = 6, 2, 6
STEPS = 16
NT = (((1,), (1,)), ((), ()))


def dot(a, b):
    return jnp.dot(a, b, preferred_element_type=F32)


def dot_nt(a, b):
    return lax.dot_general(a, b, NT, preferred_element_type=F32)


def copy_to(src, dst, send, recv, sp, dp):
    return pltpu.make_async_remote_copy(
        src_ref=src, dst_ref=dst, send_sem=send, recv_sem=recv,
        device_id={"sp": sp, "dp": dp}, device_id_type=MESH,
    )


def place():
    sp = lax.axis_index("sp")
    g = lax.axis_index("dp")
    z = sp // 4
    x = sp % 4
    return z, x, g, g // 2, g % 2


def signal(sem, sp, dp):
    pl.semaphore_signal(sem, inc=1, device_id={"sp": sp, "dp": dp}, device_id_type=MESH)


def route(idst, rwt, d_ref, c_ref):
    slots = 64 * SLOT
    order = (idst & 31) * 2 + (idst >> 5)
    coef = rwt / jnp.sum(rwt, axis=0, keepdims=True)
    hits = jnp.zeros((64, TOK), F32)
    weights = jnp.zeros((64, TOK), F32)
    expert = lax.broadcasted_iota(jnp.int32, (64, TOK), 0)
    for k in range(idst.shape[0]):
        hit = order[k : k + 1, :] == expert
        hits = hits + jnp.where(hit, 1.0, 0.0)
        weights = weights + jnp.where(hit, coef[k : k + 1, :], 0.0)
    r = lax.broadcasted_iota(jnp.int32, (TOK, TOK), 0)
    q = lax.broadcasted_iota(jnp.int32, (TOK, TOK), 1)
    earlier = jnp.where(r < q, 1.0, 0.0).astype(BF16)
    hits = hits.astype(BF16)
    before = dot(hits, earlier).astype(BF16)
    hi = weights.astype(BF16)
    lo = (weights - hi.astype(F32)).astype(BF16)
    for b in range(slots // 256):
        s0 = lax.broadcasted_iota(jnp.int32, (256, 64), 0) + b * 256
        e1 = lax.broadcasted_iota(jnp.int32, (256, 64), 1)
        rep = jnp.where((s0 >> 4) == e1, 1.0, 0.0).astype(BF16)
        lane = (lax.broadcasted_iota(jnp.int32, (256, TOK), 0) & 15).astype(F32)
        keep = jnp.where(dot(rep, hits) > 0.5, jnp.where(dot(rep, before) == lane, 1.0, 0.0), 0.0)
        at = slice(b * 256, (b + 1) * 256)
        d_ref[at, :] = keep.astype(BF16)
        c_ref[0:TOK, at] = jnp.transpose(dot(rep, hi) * keep).astype(BF16)
        c_ref[TOK : 2 * TOK, at] = jnp.transpose(dot(rep, lo) * keep).astype(BF16)


def layer_kernel(
    q_hbm, k_hbm, v_hbm, qg_hbm, kg_hbm, cos_hbm, sin_hbm, wt_hbm,
    hid_hbm, gain_hbm, idst_hbm, rwt_hbm, gate_ref, up_ref, down_ref,
    out_ref,
    q_ref, k_ref, v_ref, qg_ref, kg_ref, cos_ref, sin_ref, wt_ref,
    hid_ref, gain_ref, idst_ref, rwt_ref, d_ref, c_ref, in_sem,
    qsend, kvsend, qbuf, qall, kvbuf, acc, den, ctx, wz, wfull, pstage, pbuf,
    resid, outb, inb, yb, retb, wg, wu, wd,
    q_s, q_r, kv_s, kv_r, up_s, up_r, dn_s, dn_r, sib_s, sib_r, wz_s, wz_r, wf_s, wf_r, p_s, p_r,
    own_sem, wup_s, wup_r, wdn_s, wdn_r, loc, a_s, a_r, b_s, b_r,
):
    z, x, g, y, c = place()
    sp = z * 4 + x
    q_idx = g * 4 + x
    up_sp = ((z + 1) % ZN) * 4 + x
    dn_sp = ((z + ZN - 1) % ZN) * 4 + x
    sib = y * 2 + (1 - c)
    is_self = c == x // 2
    own_k = z // 8
    source = z % 8 == g
    inner = jnp.logical_not(source)
    p_ring = (z - g + ZN) % ZN

    pairs = (
        (q_hbm, q_ref), (k_hbm, k_ref), (v_hbm, v_ref), (qg_hbm, qg_ref), (kg_hbm, kg_ref), (cos_hbm, cos_ref),
        (sin_hbm, sin_ref), (wt_hbm, wt_ref), (hid_hbm, hid_ref), (gain_hbm, gain_ref), (idst_hbm, idst_ref),
        (rwt_hbm, rwt_ref),
    )
    loads = [pltpu.make_async_copy(src, dst, in_sem.at[i]) for i, (src, dst) in enumerate(pairs)]
    for load in loads:
        load.start()
    barrier = pltpu.get_barrier_semaphore()

    def loop(lo, hi, fn):
        def one(i, carry):
            fn(i)
            return carry

        lax.fori_loop(lo, hi, one, 0)

    loop(1, ZN, lambda o: signal(barrier, ((z + o) % ZN) * 4 + x, g))

    def slice_peer(o):
        t = (q_idx + o) % 32
        return t, z * 4 + t % 4, t // 4

    def greet(o):
        t, psp, pdp = slice_peer(o)
        signal(barrier, psp, pdp)

    loop(1, 32, greet)

    stores = (wg, wu, wd)
    own = [
        pltpu.make_async_copy(src, dst.at[own_k], own_sem.at[i])
        for i, (src, dst) in enumerate(zip((gate_ref, up_ref, down_ref), stores))
    ]

    @pl.when(source)
    def _():
        for copy in own:
            copy.start()

    for i in (1, 2, 4, 5, 6):
        loads[i].wait()
    cosv = cos_ref[...]
    sinv = sin_ref[...]

    def turned(val, gain):
        val = val.astype(F32)
        ms = jnp.mean(val * val, axis=-1, keepdims=True)
        n = val * lax.rsqrt(ms + EPS) * gain
        return (n * cosv + pltpu.roll(n, 64, 1) * sinv).astype(BF16)

    for h in range(2):
        kvsend[h, :, 0:128] = turned(k_ref[:, h * 128 : (h + 1) * 128], kg_ref[...])
        kvsend[h, :, 128:256] = v_ref[:, h * 128 : (h + 1) * 128]
    pl.semaphore_wait(barrier, 46)

    k_up = p_ring // 8
    k_dn = jnp.where(source, k_up, 1 - k_up)
    k_up_in = ((p_ring + ZN - 1) % ZN) // 8
    far_up = p_ring % 8
    far_dn = (ZN - p_ring) % 8
    down = far_dn != 7

    hop = p_ring % 8

    def wz_copy(n, k, shift):
        ref = wz.at[k]
        return copy_to(ref, ref, wz_s.at[n], wz_r.at[k], ((z + shift + ZN) % ZN) * 4 + x, g)

    routes = ((0, k_up, (2, 5, -2, -5)), (2, k_up, (-1, 1)), (5, k_up, (-1, 1, 2, 3)), (6, k_dn, (1, -1)), (3, k_dn, (1, -1, -2)))

    def wz_wait(k):
        pltpu.make_async_copy(wz.at[k], wz.at[k], wz_r.at[k]).wait()

    def wz_run(which, fn):
        for at, k, shifts in which:

            @pl.when(hop == at)
            def _():
                for n, shift in enumerate(shifts):
                    fn(wz_copy(n, k, shift))

    def piece(j, fn):
        at = 0
        for store, (n_rows, count) in zip(stores, PIECES):
            first = at

            @pl.when(jnp.logical_and(j >= first, j < first + count))
            def _():
                start = pl.multiple_of((j - first) * n_rows, n_rows)
                fn(lambda k: store.at[k, pl.ds(start, n_rows), :])

            at += count

    def wup(ref, j):
        return copy_to(ref, ref, wup_s.at[j], wup_r.at[j], up_sp, g)

    def wdn(ref, j):
        return copy_to(ref, ref, wdn_s.at[j], wdn_r.at[j], dn_sp, g)

    def one_up(j):
        def act(ref):
            @pl.when(inner)
            def _():
                wup(ref(k_up_in), j).wait_recv()

            wup(ref(k_up), j).start()

        piece(j, act)

    def one_dn(j):
        def act(ref):
            @pl.when(inner)
            def _():
                wdn(ref(k_dn), j).wait_recv()

            @pl.when(down)
            def _():
                wdn(ref(k_dn), j).start()

        piece(j, act)

    def reach(t, far):
        return jnp.clip(FIRST + PER_STEP * t - LAG * far // 2, 0, NPIECE)

    def ring(t):
        for far, act in ((far_up, one_up), (far_dn, one_dn)):
            lo = jnp.where(jnp.logical_and(t == 0, inner), 0, reach(t, far))
            loop(lo, reach(t + 1, far), act)


    rows = pl.ds(pl.multiple_of((x % 2) * TOK, TOK), TOK)
    dest_dp = y * 2 + x // 2

    def to_chip(h, src, dst, send, recv):
        here = jnp.logical_and(is_self, x % 2 == h)

        @pl.when(here)
        def _():
            pltpu.make_async_copy(src, dst, recv).start()

        @pl.when(jnp.logical_not(here))
        def _():
            copy_to(src, dst, send, recv, z * 4 + 2 * c + h, dest_dp).start()

    for h in range(2):
        to_chip(h, kvsend.at[h], kvbuf.at[z, x // 2, rows, :], kv_s.at[h], kv_r.at[x % 2])
    loads[7].wait()

    @pl.when(source)
    def _():
        wz[own_k] = wt_ref[...]

    wz_run(routes[:1], lambda copy: copy.start())
    @pl.when(source)
    def _():
        for copy in own:
            copy.wait()
        loop(0, FIRST, one_up)
        loop(0, FIRST, one_dn)

    for i in (0, 3, 8, 9, 10, 11):
        loads[i].wait()
    for h in range(2):
        for n in range(8):
            at = (h * 8 + n) * 128
            qsend[h, :, n * 128 : (n + 1) * 128] = turned(q_ref[:, at : at + 128], qg_ref[...])
        to_chip(h, qsend.at[h], qbuf.at[x % 2], q_s.at[h], q_r.at[x % 2])

    route(idst_ref[...], rwt_ref[...], d_ref, c_ref)
    for n in range(1, 5):
        at, k, _ = routes[n]

        @pl.when(hop == at)
        def _():
            wz_wait(k)

    wz_run(routes[1:], lambda copy: copy.start())
    ring(0)

    for t in range(2):
        kdst = kvbuf.at[z, c, pl.ds(t * TOK, TOK), :]
        pltpu.make_async_copy(kdst, kdst, kv_r.at[t]).wait()

    def up_copy(s, slice_idx):
        ref = kvbuf.at[slice_idx, c]
        return copy_to(ref, ref, up_s.at[s], up_r.at[s], up_sp, g)

    def dn_copy(s, slice_idx):
        ref = kvbuf.at[slice_idx, c]
        return copy_to(ref, ref, dn_s.at[s], dn_r.at[s], dn_sp, g)

    def sib_copy(i, slice_idx, half):
        ref = kvbuf.at[slice_idx, half]
        return copy_to(ref, ref, sib_s.at[i], sib_r.at[i], sp, sib)

    @pl.when(z < ZN - 1)
    def _():
        up_copy(1, z).start()

    @pl.when(z <= 6)
    def _():
        dn_copy(1, z).start()

    sib_copy(0, z, c).start()

    for t in range(2):
        pltpu.make_async_copy(qbuf.at[t], qbuf.at[t], q_r.at[t]).wait()
    for n in range(8):
        for t in range(2):
            qall[n * 192 + t * TOK : n * 192 + (t + 1) * TOK, :] = qbuf[t, :, n * 128 : (n + 1) * 128]

    ring(1)
    factor = math.log2(math.e) / math.sqrt(128)

    def attend(slice_idx, diagonal):
        kv = kvbuf[slice_idx]
        kk = kv[:, :, 0:128].reshape(384, 128)
        vv = kv[:, :, 128:256].reshape(384, 128)
        for n in range(4):
            at = slice(n * 384, (n + 1) * 384)
            s = dot_nt(qall[at, :], kk)
            p = jnp.exp2(s * factor)
            if diagonal:
                r = lax.broadcasted_iota(jnp.int32, (384, 384), 0)
                r = jnp.where(r >= 192, r - 192, r) + c * 192
                col = lax.broadcasted_iota(jnp.int32, (384, 384), 1)
                p = jnp.where(col <= r, p, 0.0)
            part = p[:, 0:128] + p[:, 128:256] + p[:, 256:384]
            pv = dot(p.astype(BF16), vv)
            if diagonal:
                den[at, :] = part
                acc[at, :] = pv
            else:
                den[at, :] = den[at, :] + part
                acc[at, :] = acc[at, :] + pv

    relay_up = jnp.logical_or(hop == 2, hop == 5)
    relay_dn = jnp.logical_or(hop == 3, hop == 6)
    @pl.when(relay_up)
    def _():
        wz_wait(k_dn)

    @pl.when(relay_dn)
    def _():
        wz_wait(k_up)

    @pl.when(source)
    def _():
        wz_wait(1 - own_k)

    @pl.when(jnp.logical_not(jnp.logical_or(source, jnp.logical_or(relay_up, relay_dn))))
    def _():
        wz_wait(0)
        wz_wait(1)

    def wf_copy(o):
        t = (y * 4 + x + o) % 16
        cols = pl.ds(pl.multiple_of((t % 2) * 1024, 1024), 1024)
        return copy_to(
            wz.at[:, :, cols], wfull.at[:, y, c, x], wf_s.at[o], wf_r.at[o], z * 4 + t % 4, (t // 4) * 2 + c
        )

    def wf_sib(half):
        ref = wfull.at[:, :, half]
        return copy_to(ref, ref, wf_s.at[0], wf_r.at[0], sp, sib)

    loop(1, 16, lambda o: wf_copy(o).start())
    mine = pl.ds(pl.multiple_of((x % 2) * 1024, 1024), 1024)
    local = pltpu.make_async_copy(wz.at[:, :, mine], wfull.at[:, y, c, x], loc.at[0])
    local.start()

    sib_copy(0, z, 1 - c).wait_recv()
    attend(z, True)
    ring(2)

    def step(s):
        below = (z - s + ZN) % ZN
        above = (z + s) % ZN
        from_below = z >= s
        above_on = jnp.logical_and(s < 8, jnp.logical_or(z + s <= 6, z + s >= ZN))
        above_used = jnp.logical_and(s < 8, z + s >= ZN)

        @pl.when(from_below)
        def _():
            up_copy(s, below).wait_recv()

            @pl.when(jnp.logical_and(s < 8, z < ZN - 1))
            def _():
                up_copy(s + 1, below).start()

            sib_copy(2 * s, below, c).start()

        @pl.when(above_on)
        def _():
            dn_copy(s, above).wait_recv()

            @pl.when(s < 7)
            def _():
                dn_copy(s + 1, above).start()

        @pl.when(above_used)
        def _():
            sib_copy(2 * s + 1, above, c).start()

        ring(s + 2)

        @pl.when(from_below)
        def _():
            sib_copy(2 * s, below, 1 - c).wait_recv()
            attend(below, False)

        @pl.when(above_used)
        def _():
            sib_copy(2 * s + 1, above, 1 - c).wait_recv()
            attend(above, False)

    loop(1, 6, step)
    loop(1, 16, lambda o: wf_copy(o).wait_recv())
    local.wait()
    wf_sib(c).start()
    loop(6, 9, step)

    for n in range(8):
        at = slice(n * 192, (n + 1) * 192)
        total = jnp.sum(den[at, :], axis=-1, keepdims=True)
        ctx[:, n * 128 : (n + 1) * 128] = (acc[at, :] / total).astype(BF16)
    ring(11)
    wf_sib(1 - c).wait_recv()
    for b in range(4):
        w = wfull[b // 2, (b % 2) * 2 : (b % 2 + 1) * 2].reshape(256, 1024)
        part = dot_nt(ctx[...], w).astype(BF16)
        for t in range(2):
            pstage[t, :, b * 256 : (b + 1) * 256] = part[t * TOK : (t + 1) * TOK, :]
    for t in range(2):
        to_chip(t, pstage.at[t], pbuf.at[x % 2], p_s.at[t], p_r.at[x % 2])

    loop(12, STEPS, ring)
    for h in range(2):
        pltpu.make_async_copy(pbuf.at[h], pbuf.at[h], p_r.at[h]).wait()

    attn = (pbuf[0].astype(F32) + pbuf[1].astype(F32)).astype(BF16).astype(F32)
    res = hid_ref[...].astype(F32) + attn
    resid[...] = res
    ms = jnp.mean(res * res, axis=-1, keepdims=True)
    normed = (res * lax.rsqrt(ms + EPS) * gain_ref[...]).astype(BF16)

    def first_of(dp):
        return (((z - dp + ZN) % ZN + 3) // 8) % 2

    def there(o, r):
        t, psp, pdp = slice_peer(o)
        kk = (first_of(pdp) + r) % 2
        return copy_to(outb.at[t, kk], inb.at[kk, q_idx], a_s.at[r, o], a_r.at[r, o], psp, pdp)

    def back(o, r):
        t, psp, pdp = slice_peer(o)
        kk = (first_of(g) + r) % 2
        return copy_to(yb.at[kk, t], retb.at[q_idx, kk], b_s.at[r, o], b_r.at[r, o], psp, pdp)

    def run_expert(r):
        kk = (first_of(g) + r) % 2
        loop(1, 32, lambda o: there(o, r).wait_recv())
        tokens = inb[kk].reshape(512, 1024)
        gate = dot(tokens, wg[kk])
        upv = dot(tokens, wu[kk])
        mid = (gate / (1.0 + jnp.exp(-gate)) * upv).astype(BF16)
        yb[kk] = dot(mid, wd[kk]).astype(BF16).reshape(32, SLOT, 1024)
        loop(1, 32, lambda o: back(o, r).start())
        keep = pltpu.make_async_copy(yb.at[kk, q_idx], retb.at[q_idx, kk], loc.at[2 + r])
        keep.start()
        return keep

    for b in range(4):
        part = dot(d_ref[b * 256 : (b + 1) * 256, :], normed).astype(BF16)
        outb[b * 8 : (b + 1) * 8] = part.reshape(8, 2, SLOT, 1024)
    loop(1, 32, lambda o: there(o, 0).start())
    loop(1, 32, lambda o: there(o, 1).start())
    keep = pltpu.make_async_copy(outb.at[q_idx], inb.at[:, q_idx], loc.at[1])
    keep.start()

    def rest(i):
        for far, act in ((far_up, one_up), (far_dn, one_dn)):
            j = i - LAG * far // 2

            @pl.when(jnp.logical_and(j >= 0, j < NPIECE))
            def _():
                act(j)

    loop(FIRST + PER_STEP * STEPS, NPIECE + LAG * 2, rest)
    keep.wait()
    keep_first = run_expert(0)
    loop(NPIECE + LAG * 2, NPIECE + LAG * 7 // 2, rest)

    @pl.when(source)
    def _():
        loop(0, NPIECE, lambda j: piece(j, lambda ref: wup(ref(k_up_in), j).wait_recv()))

    keep_second = run_expert(1)

    wz_run(routes, lambda copy: copy.wait_send())
    loop(0, NPIECE, lambda j: piece(j, lambda ref: wup(ref(k_up), j).wait_send()))

    @pl.when(down)
    def _():
        loop(0, NPIECE, lambda j: piece(j, lambda ref: wdn(ref(k_dn), j).wait_send()))

    loop(1, 16, lambda o: wf_copy(o).wait_send())
    wf_sib(c).wait_send()

    def kv_sent(s):
        @pl.when(jnp.logical_and(z >= s - 1, z < ZN - 1))
        def _():
            up_copy(s, z).wait_send()

        @pl.when(jnp.logical_and(s < 8, jnp.logical_or(z + s <= 7, z + s >= ZN + 1)))
        def _():
            dn_copy(s, z).wait_send()

        @pl.when(z >= s)
        def _():
            sib_copy(2 * s, z, c).wait_send()

        @pl.when(jnp.logical_and(s < 8, z + s >= ZN))
        def _():
            sib_copy(2 * s + 1, z, c).wait_send()

    sib_copy(0, z, c).wait_send()
    loop(1, 9, kv_sent)
    for h in range(2):
        here = jnp.logical_and(is_self, x % 2 == h)

        @pl.when(jnp.logical_not(here))
        def _():
            dst = kvbuf.at[z, x // 2, rows, :]
            dest_sp = z * 4 + 2 * c + h
            copy_to(kvsend.at[h], dst, kv_s.at[h], kv_r.at[x % 2], dest_sp, dest_dp).wait_send()
            copy_to(qsend.at[h], qbuf.at[x % 2], q_s.at[h], q_r.at[x % 2], dest_sp, dest_dp).wait_send()
            copy_to(pstage.at[h], pbuf.at[x % 2], p_s.at[h], p_r.at[x % 2], dest_sp, dest_dp).wait_send()

    for r in range(2):
        loop(1, 32, lambda o, r=r: there(o, r).wait_send())
    keep_first.wait()
    keep_second.wait()
    for r in range(2):
        loop(1, 32, lambda o, r=r: back(o, r).wait_recv())
    mixed = dot(c_ref[...], retb[...].reshape(1024, 1024))
    out_ref[...] = (resid[...] + (mixed[0:TOK, :] + mixed[TOK : 2 * TOK, :])).astype(BF16)
    for r in range(2):
        loop(1, 32, lambda o, r=r: back(o, r).wait_send())


def body(
    hidden_in, queries, keys, values, q_gain, k_gain, out_weight, moe_gain,
    expert_ids, route_weights, gate_proj, up_proj, down_proj,
):
    sp = lax.axis_index("sp")
    positions = sp * TOK + jnp.arange(TOK, dtype=jnp.int32)
    expo = jnp.arange(64).astype(F32) * (-2.0 / 128)
    freq = jnp.power(jnp.float32(THETA), expo)
    angle = positions.astype(F32)[:, None] * freq[None, :]
    cosv = jnp.cos(angle)
    sinv = jnp.sin(angle)
    cos2 = jnp.concatenate([cosv, cosv], axis=-1)
    sin2 = jnp.concatenate([-sinv, sinv], axis=-1)
    vm = pl.BlockSpec(memory_space=pltpu.VMEM)
    hbm = pl.BlockSpec(memory_space=pltpu.HBM)
    dma = pltpu.SemaphoreType.DMA

    return pl.pallas_call(
        layer_kernel,
        out_shape=jax.ShapeDtypeStruct((TOK, 1024), BF16),
        in_specs=[hbm] * 15,
        out_specs=vm,
        scratch_shapes=[
            pltpu.VMEM((TOK, 2048), BF16),
            pltpu.VMEM((TOK, 256), BF16),
            pltpu.VMEM((TOK, 256), BF16),
            pltpu.VMEM((1, 128), F32),
            pltpu.VMEM((1, 128), F32),
            pltpu.VMEM((TOK, 128), F32),
            pltpu.VMEM((TOK, 128), F32),
            pltpu.VMEM((16, 2048), BF16),
            pltpu.VMEM((TOK, 1024), BF16),
            pltpu.VMEM((1, 1024), F32),
            pltpu.VMEM((8, TOK), jnp.int32),
            pltpu.VMEM((8, TOK), F32),
            pltpu.VMEM((64 * SLOT, TOK), BF16),
            pltpu.VMEM((2 * TOK, 64 * SLOT), BF16),
            dma((12,)),
            pltpu.VMEM((2, TOK, 1024), BF16),
            pltpu.VMEM((2, TOK, 256), BF16),
            pltpu.VMEM((2, TOK, 1024), BF16),
            pltpu.VMEM((1536, 128), BF16),
            pltpu.VMEM((ZN, 2, 192, 256), BF16),
            pltpu.VMEM((1536, 128), F32),
            pltpu.VMEM((1536, 128), F32),
            pltpu.VMEM((192, 1024), BF16),
            pltpu.VMEM((2, 16, 2048), BF16),
            pltpu.VMEM((2, 4, 2, 4, 16, 1024), BF16),
            pltpu.VMEM((2, TOK, 1024), BF16),
            pltpu.VMEM((2, TOK, 1024), BF16),
            pltpu.VMEM((TOK, 1024), F32),
            pltpu.VMEM((32, 2, SLOT, 1024), BF16),
            pltpu.VMEM((2, 32, SLOT, 1024), BF16),
            pltpu.VMEM((2, 32, SLOT, 1024), BF16),
            pltpu.VMEM((32, 2, SLOT, 1024), BF16),
            pltpu.VMEM((2, 1024, 384), BF16),
            pltpu.VMEM((2, 1024, 384), BF16),
            pltpu.VMEM((2, 384, 1024), BF16),
            dma((2,)), dma((2,)), dma((2,)), dma((2,)),
            dma((9,)), dma((9,)), dma((9,)), dma((9,)),
            dma((17,)), dma((17,)),
            dma((4,)), dma((2,)), dma((16,)), dma((16,)),
            dma((2,)), dma((2,)), dma((4,)),
            dma((NPIECE,)), dma((NPIECE,)), dma((NPIECE,)), dma((NPIECE,)),
            dma((4,)),
            dma((2, 32)), dma((2, 32)), dma((2, 32)), dma((2, 32)),
        ],
        compiler_params=pltpu.CompilerParams(
            collective_id=0, has_side_effects=True, vmem_limit_bytes=63 * 1024 * 1024
        ),
        name="layer",
    )(
        queries, keys, values, q_gain.reshape(1, 128), k_gain.reshape(1, 128), cos2, sin2, out_weight.T,
        hidden_in, moe_gain.reshape(1, 1024), expert_ids.T, route_weights.T, gate_proj[0], up_proj[0], down_proj[0],
    )


def solution(mesh):
    tok = P(("dp", "sp"), None)
    return jax.shard_map(
        body,
        mesh=mesh,
        in_specs=(
            tok, tok, tok, tok, P(), P(), P(None, "sp"), P(), tok, tok,
            P("sp", None, None), P("sp", None, None), P("sp", None, None),
        ),
        out_specs=tok,
        check_vma=False,
    )
```

```python
import functools
import math

import jax
import jax.numpy as jnp
from jax import lax
from jax.experimental import pallas as pl
from jax.experimental.pallas import tpu as pltpu
from jax.sharding import PartitionSpec as P

EPS = 1e-06
THETA = 1000000.0
MESH = pl.DeviceIdType.MESH
F32 = jnp.float32
BF16 = jnp.bfloat16

TOK = 96
ZN = 16
SLOT = 16
PIECES = ((128, 8), (128, 8), (64, 6))
NPIECE = 22
FIRST, PER_STEP, LAG = 4, 1, 4
STEPS = 16
NT = (((1,), (1,)), ((), ()))


def dot(a, b):
    return jnp.dot(a, b, preferred_element_type=F32)


def dot_nt(a, b):
    return lax.dot_general(a, b, NT, preferred_element_type=F32)


def copy_to(src, dst, send, recv, sp, dp):
    return pltpu.make_async_remote_copy(
        src_ref=src, dst_ref=dst, send_sem=send, recv_sem=recv,
        device_id={"sp": sp, "dp": dp}, device_id_type=MESH,
    )


def place():
    sp = lax.axis_index("sp")
    g = lax.axis_index("dp")
    z = sp // 4
    x = sp % 4
    return z, x, g, g // 2, g % 2


def signal(sem, sp, dp):
    pl.semaphore_signal(sem, inc=1, device_id={"sp": sp, "dp": dp}, device_id_type=MESH)


def route(idst, rwt, d_ref, c_ref):
    slots = 64 * SLOT
    order = (idst & 31) * 2 + (idst >> 5)
    coef = rwt / jnp.sum(rwt, axis=0, keepdims=True)
    hits = jnp.zeros((64, TOK), F32)
    weights = jnp.zeros((64, TOK), F32)
    expert = lax.broadcasted_iota(jnp.int32, (64, TOK), 0)
    for k in range(idst.shape[0]):
        hit = order[k : k + 1, :] == expert
        hits = hits + jnp.where(hit, 1.0, 0.0)
        weights = weights + jnp.where(hit, coef[k : k + 1, :], 0.0)
    r = lax.broadcasted_iota(jnp.int32, (TOK, TOK), 0)
    q = lax.broadcasted_iota(jnp.int32, (TOK, TOK), 1)
    earlier = jnp.where(r < q, 1.0, 0.0).astype(BF16)
    hits = hits.astype(BF16)
    before = dot(hits, earlier).astype(BF16)
    hi = weights.astype(BF16)
    lo = (weights - hi.astype(F32)).astype(BF16)
    for b in range(slots // 256):
        s0 = lax.broadcasted_iota(jnp.int32, (256, 64), 0) + b * 256
        e1 = lax.broadcasted_iota(jnp.int32, (256, 64), 1)
        rep = jnp.where((s0 >> 4) == e1, 1.0, 0.0).astype(BF16)
        lane = (lax.broadcasted_iota(jnp.int32, (256, TOK), 0) & 15).astype(F32)
        keep = jnp.where(dot(rep, hits) > 0.5, jnp.where(dot(rep, before) == lane, 1.0, 0.0), 0.0)
        at = slice(b * 256, (b + 1) * 256)
        d_ref[at, :] = keep.astype(BF16)
        c_ref[0:TOK, at] = jnp.transpose(dot(rep, hi) * keep).astype(BF16)
        c_ref[TOK : 2 * TOK, at] = jnp.transpose(dot(rep, lo) * keep).astype(BF16)


def layer_kernel(
    q_hbm, k_hbm, v_hbm, qg_hbm, kg_hbm, cos_hbm, sin_hbm, wt_hbm,
    hid_hbm, gain_hbm, idst_hbm, rwt_hbm, gate_ref, up_ref, down_ref,
    out_ref,
    q_ref, k_ref, v_ref, qg_ref, kg_ref, cos_ref, sin_ref, wt_ref,
    hid_ref, gain_ref, idst_ref, rwt_ref, d_ref, c_ref, in_sem,
    qsend, kvsend, qbuf, qall, kvbuf, acc, den, ctx, wz, wfull, pstage, pbuf,
    resid, outb, inb, yb, retb, wg, wu, wd,
    q_s, q_r, kv_s, kv_r, up_s, up_r, dn_s, dn_r, sib_s, sib_r, wz_s, wz_r, wf_s, wf_r, p_s, p_r,
    own_sem, wup_s, wup_r, wdn_s, wdn_r, loc, a_s, a_r, b_s, b_r,
):
    z, x, g, y, c = place()
    sp = z * 4 + x
    q_idx = g * 4 + x
    up_sp = ((z + 1) % ZN) * 4 + x
    dn_sp = ((z + ZN - 1) % ZN) * 4 + x
    sib = y * 2 + (1 - c)
    is_self = c == x // 2
    own_k = z // 8
    source = z % 8 == g
    inner = jnp.logical_not(source)
    p_ring = (z - g + ZN) % ZN

    pairs = (
        (q_hbm, q_ref), (k_hbm, k_ref), (v_hbm, v_ref), (qg_hbm, qg_ref), (kg_hbm, kg_ref), (cos_hbm, cos_ref),
        (sin_hbm, sin_ref), (wt_hbm, wt_ref), (hid_hbm, hid_ref), (gain_hbm, gain_ref), (idst_hbm, idst_ref),
        (rwt_hbm, rwt_ref),
    )
    loads = [pltpu.make_async_copy(src, dst, in_sem.at[i]) for i, (src, dst) in enumerate(pairs)]
    for load in loads:
        load.start()
    barrier = pltpu.get_barrier_semaphore()

    def loop(lo, hi, fn):
        def one(i, carry):
            fn(i)
            return carry

        lax.fori_loop(lo, hi, one, 0)

    loop(1, ZN, lambda o: signal(barrier, ((z + o) % ZN) * 4 + x, g))

    def slice_peer(o):
        t = (q_idx + o) % 32
        return t, z * 4 + t % 4, t // 4

    def greet(o):
        t, psp, pdp = slice_peer(o)
        signal(barrier, psp, pdp)

    loop(1, 32, greet)

    stores = (wg, wu, wd)
    own = [
        pltpu.make_async_copy(src, dst.at[own_k], own_sem.at[i])
        for i, (src, dst) in enumerate(zip((gate_ref, up_ref, down_ref), stores))
    ]

    @pl.when(source)
    def _():
        for copy in own:
            copy.start()

    for i in (1, 2, 4, 5, 6):
        loads[i].wait()
    cosv = cos_ref[...]
    sinv = sin_ref[...]

    def turned(val, gain):
        val = val.astype(F32)
        ms = jnp.mean(val * val, axis=-1, keepdims=True)
        n = val * lax.rsqrt(ms + EPS) * gain
        return (n * cosv + pltpu.roll(n, 64, 1) * sinv).astype(BF16)

    for h in range(2):
        kvsend[h, :, 0:128] = turned(k_ref[:, h * 128 : (h + 1) * 128], kg_ref[...])
        kvsend[h, :, 128:256] = v_ref[:, h * 128 : (h + 1) * 128]
    pl.semaphore_wait(barrier, 46)

    k_up = p_ring // 8
    k_dn = jnp.where(source, k_up, 1 - k_up)
    k_up_in = ((p_ring + ZN - 1) % ZN) // 8
    far_up = p_ring % 8
    far_dn = (ZN - p_ring) % 8
    down = far_dn != 7

    hop = p_ring % 8

    def wz_copy(n, k, shift):
        ref = wz.at[k]
        return copy_to(ref, ref, wz_s.at[n], wz_r.at[k], ((z + shift + ZN) % ZN) * 4 + x, g)

    routes = ((0, k_up, (2, 5, -2, -5)), (2, k_up, (-1, 1)), (5, k_up, (-1, 1, 2, 3)), (6, k_dn, (1, -1)), (3, k_dn, (1, -1, -2)))

    def wz_wait(k):
        pltpu.make_async_copy(wz.at[k], wz.at[k], wz_r.at[k]).wait()

    def wz_run(which, fn):
        for at, k, shifts in which:

            @pl.when(hop == at)
            def _():
                for n, shift in enumerate(shifts):
                    fn(wz_copy(n, k, shift))

    def piece(j, fn):
        at = 0
        for store, (n_rows, count) in zip(stores, PIECES):
            first = at

            @pl.when(jnp.logical_and(j >= first, j < first + count))
            def _():
                start = pl.multiple_of((j - first) * n_rows, n_rows)
                fn(lambda k: store.at[k, pl.ds(start, n_rows), :])

            at += count

    def wup(ref, j):
        return copy_to(ref, ref, wup_s.at[j], wup_r.at[j], up_sp, g)

    def wdn(ref, j):
        return copy_to(ref, ref, wdn_s.at[j], wdn_r.at[j], dn_sp, g)

    def one_up(j):
        def act(ref):
            @pl.when(inner)
            def _():
                wup(ref(k_up_in), j).wait_recv()

            wup(ref(k_up), j).start()

        piece(j, act)

    def one_dn(j):
        def act(ref):
            @pl.when(inner)
            def _():
                wdn(ref(k_dn), j).wait_recv()

            @pl.when(down)
            def _():
                wdn(ref(k_dn), j).start()

        piece(j, act)

    def reach(t, far):
        return jnp.clip(FIRST + PER_STEP * t - LAG * far // 2, 0, NPIECE)

    def ring(t):
        for far, act in ((far_up, one_up), (far_dn, one_dn)):
            lo = jnp.where(jnp.logical_and(t == 0, inner), 0, reach(t, far))
            loop(lo, reach(t + 1, far), act)


    rows = pl.ds(pl.multiple_of((x % 2) * TOK, TOK), TOK)
    dest_dp = y * 2 + x // 2

    def to_chip(h, src, dst, send, recv):
        here = jnp.logical_and(is_self, x % 2 == h)

        @pl.when(here)
        def _():
            pltpu.make_async_copy(src, dst, recv).start()

        @pl.when(jnp.logical_not(here))
        def _():
            copy_to(src, dst, send, recv, z * 4 + 2 * c + h, dest_dp).start()

    for h in range(2):
        to_chip(h, kvsend.at[h], kvbuf.at[z, x // 2, rows, :], kv_s.at[h], kv_r.at[x % 2])
    loads[7].wait()

    @pl.when(source)
    def _():
        wz[own_k] = wt_ref[...]

    wz_run(routes[:1], lambda copy: copy.start())
    @pl.when(source)
    def _():
        for copy in own:
            copy.wait()
        loop(0, FIRST, one_up)
        loop(0, FIRST, one_dn)

    for i in (0, 3, 8, 9, 10, 11):
        loads[i].wait()
    for h in range(2):
        for n in range(8):
            at = (h * 8 + n) * 128
            qsend[h, :, n * 128 : (n + 1) * 128] = turned(q_ref[:, at : at + 128], qg_ref[...])
        to_chip(h, qsend.at[h], qbuf.at[x % 2], q_s.at[h], q_r.at[x % 2])

    route(idst_ref[...], rwt_ref[...], d_ref, c_ref)
    for n in range(1, 5):
        at, k, _ = routes[n]

        @pl.when(hop == at)
        def _():
            wz_wait(k)

    wz_run(routes[1:], lambda copy: copy.start())
    ring(0)

    for t in range(2):
        kdst = kvbuf.at[z, c, pl.ds(t * TOK, TOK), :]
        pltpu.make_async_copy(kdst, kdst, kv_r.at[t]).wait()

    def up_copy(s, slice_idx):
        ref = kvbuf.at[slice_idx, c]
        return copy_to(ref, ref, up_s.at[s], up_r.at[s], up_sp, g)

    def dn_copy(s, slice_idx):
        ref = kvbuf.at[slice_idx, c]
        return copy_to(ref, ref, dn_s.at[s], dn_r.at[s], dn_sp, g)

    def sib_copy(i, slice_idx, half):
        ref = kvbuf.at[slice_idx, half]
        return copy_to(ref, ref, sib_s.at[i], sib_r.at[i], sp, sib)

    @pl.when(z < ZN - 1)
    def _():
        up_copy(1, z).start()

    @pl.when(z <= 6)
    def _():
        dn_copy(1, z).start()

    sib_copy(0, z, c).start()

    for t in range(2):
        pltpu.make_async_copy(qbuf.at[t], qbuf.at[t], q_r.at[t]).wait()
    for n in range(8):
        for t in range(2):
            qall[n * 192 + t * TOK : n * 192 + (t + 1) * TOK, :] = qbuf[t, :, n * 128 : (n + 1) * 128]

    ring(1)
    factor = math.log2(math.e) / math.sqrt(128)

    def attend(slice_idx, diagonal):
        kv = kvbuf[slice_idx]
        kk = kv[:, :, 0:128].reshape(384, 128)
        vv = kv[:, :, 128:256].reshape(384, 128)
        for n in range(4):
            at = slice(n * 384, (n + 1) * 384)
            s = dot_nt(qall[at, :], kk)
            p = jnp.exp2(s * factor)
            if diagonal:
                r = lax.broadcasted_iota(jnp.int32, (384, 384), 0)
                r = jnp.where(r >= 192, r - 192, r) + c * 192
                col = lax.broadcasted_iota(jnp.int32, (384, 384), 1)
                p = jnp.where(col <= r, p, 0.0)
            part = p[:, 0:128] + p[:, 128:256] + p[:, 256:384]
            pv = dot(p.astype(BF16), vv)
            if diagonal:
                den[at, :] = part
                acc[at, :] = pv
            else:
                den[at, :] = den[at, :] + part
                acc[at, :] = acc[at, :] + pv

    relay_up = jnp.logical_or(hop == 2, hop == 5)
    relay_dn = jnp.logical_or(hop == 3, hop == 6)
    @pl.when(relay_up)
    def _():
        wz_wait(k_dn)

    @pl.when(relay_dn)
    def _():
        wz_wait(k_up)

    @pl.when(source)
    def _():
        wz_wait(1 - own_k)

    @pl.when(jnp.logical_not(jnp.logical_or(source, jnp.logical_or(relay_up, relay_dn))))
    def _():
        wz_wait(0)
        wz_wait(1)

    def wf_copy(o):
        t = (y * 4 + x + o) % 16
        cols = pl.ds(pl.multiple_of((t % 2) * 1024, 1024), 1024)
        return copy_to(
            wz.at[:, :, cols], wfull.at[:, y, c, x], wf_s.at[o], wf_r.at[o], z * 4 + t % 4, (t // 4) * 2 + c
        )

    def wf_sib(half):
        ref = wfull.at[:, :, half]
        return copy_to(ref, ref, wf_s.at[0], wf_r.at[0], sp, sib)

    loop(1, 16, lambda o: wf_copy(o).start())
    mine = pl.ds(pl.multiple_of((x % 2) * 1024, 1024), 1024)
    local = pltpu.make_async_copy(wz.at[:, :, mine], wfull.at[:, y, c, x], loc.at[0])
    local.start()

    sib_copy(0, z, 1 - c).wait_recv()
    attend(z, True)
    ring(2)

    def step(s):
        below = (z - s + ZN) % ZN
        above = (z + s) % ZN
        from_below = z >= s
        above_on = jnp.logical_and(s < 8, jnp.logical_or(z + s <= 6, z + s >= ZN))
        above_used = jnp.logical_and(s < 8, z + s >= ZN)

        @pl.when(from_below)
        def _():
            up_copy(s, below).wait_recv()

            @pl.when(jnp.logical_and(s < 8, z < ZN - 1))
            def _():
                up_copy(s + 1, below).start()

            sib_copy(2 * s, below, c).start()

        @pl.when(above_on)
        def _():
            dn_copy(s, above).wait_recv()

            @pl.when(s < 7)
            def _():
                dn_copy(s + 1, above).start()

        @pl.when(above_used)
        def _():
            sib_copy(2 * s + 1, above, c).start()

        ring(s + 2)

        @pl.when(from_below)
        def _():
            sib_copy(2 * s, below, 1 - c).wait_recv()
            attend(below, False)

        @pl.when(above_used)
        def _():
            sib_copy(2 * s + 1, above, 1 - c).wait_recv()
            attend(above, False)

    loop(1, 6, step)
    loop(1, 16, lambda o: wf_copy(o).wait_recv())
    local.wait()
    wf_sib(c).start()
    loop(6, 9, step)

    for n in range(8):
        at = slice(n * 192, (n + 1) * 192)
        total = jnp.sum(den[at, :], axis=-1, keepdims=True)
        ctx[:, n * 128 : (n + 1) * 128] = (acc[at, :] / total).astype(BF16)
    ring(11)
    wf_sib(1 - c).wait_recv()
    for b in range(4):
        w = wfull[b // 2, (b % 2) * 2 : (b % 2 + 1) * 2].reshape(256, 1024)
        part = dot_nt(ctx[...], w).astype(BF16)
        for t in range(2):
            pstage[t, :, b * 256 : (b + 1) * 256] = part[t * TOK : (t + 1) * TOK, :]
    for t in range(2):
        to_chip(t, pstage.at[t], pbuf.at[x % 2], p_s.at[t], p_r.at[x % 2])

    loop(12, STEPS, ring)
    for h in range(2):
        pltpu.make_async_copy(pbuf.at[h], pbuf.at[h], p_r.at[h]).wait()

    attn = (pbuf[0].astype(F32) + pbuf[1].astype(F32)).astype(BF16).astype(F32)
    res = hid_ref[...].astype(F32) + attn
    resid[...] = res
    ms = jnp.mean(res * res, axis=-1, keepdims=True)
    normed = (res * lax.rsqrt(ms + EPS) * gain_ref[...]).astype(BF16)

    def first_of(dp):
        return (((z - dp + ZN) % ZN + 3) // 8) % 2

    def there(o, r):
        t, psp, pdp = slice_peer(o)
        kk = (first_of(pdp) + r) % 2
        return copy_to(outb.at[t, kk], inb.at[kk, q_idx], a_s.at[r, o], a_r.at[r, o], psp, pdp)

    def back(o, r):
        t, psp, pdp = slice_peer(o)
        kk = (first_of(g) + r) % 2
        return copy_to(yb.at[kk, t], retb.at[q_idx, kk], b_s.at[r, o], b_r.at[r, o], psp, pdp)

    def run_expert(r):
        kk = (first_of(g) + r) % 2
        loop(1, 32, lambda o: there(o, r).wait_recv())
        tokens = inb[kk].reshape(512, 1024)
        gate = dot(tokens, wg[kk])
        upv = dot(tokens, wu[kk])
        mid = (gate / (1.0 + jnp.exp(-gate)) * upv).astype(BF16)
        yb[kk] = dot(mid, wd[kk]).astype(BF16).reshape(32, SLOT, 1024)
        loop(1, 32, lambda o: back(o, r).start())
        keep = pltpu.make_async_copy(yb.at[kk, q_idx], retb.at[q_idx, kk], loc.at[2 + r])
        keep.start()
        return keep

    for b in range(4):
        quarter = (q_idx // 8 + b) % 4
        part = dot(d_ref[pl.ds(pl.multiple_of(quarter * 256, 256), 256), :], normed).astype(BF16)
        outb[pl.ds(quarter * 8, 8)] = part.reshape(8, 2, SLOT, 1024)

        def leave(i, quarter=quarter):
            o = (quarter * 8 + (q_idx + i) % 8 - q_idx + 32) % 32

            @pl.when(o != 0)
            def _():
                there(o, 0).start()

        loop(0, 8, leave)
    loop(1, 32, lambda o: there(o, 1).start())
    keep = pltpu.make_async_copy(outb.at[q_idx], inb.at[:, q_idx], loc.at[1])
    keep.start()

    def rest(i):
        for far, act in ((far_up, one_up), (far_dn, one_dn)):
            j = i - LAG * far // 2

            @pl.when(jnp.logical_and(j >= 0, j < NPIECE))
            def _():
                act(j)

    loop(FIRST + PER_STEP * STEPS, NPIECE + LAG * 2, rest)
    keep.wait()
    keep_first = run_expert(0)
    loop(NPIECE + LAG * 2, NPIECE + LAG * 7 // 2, rest)

    @pl.when(source)
    def _():
        loop(0, NPIECE, lambda j: piece(j, lambda ref: wup(ref(k_up_in), j).wait_recv()))

    keep_second = run_expert(1)

    wz_run(routes, lambda copy: copy.wait_send())
    loop(0, NPIECE, lambda j: piece(j, lambda ref: wup(ref(k_up), j).wait_send()))

    @pl.when(down)
    def _():
        loop(0, NPIECE, lambda j: piece(j, lambda ref: wdn(ref(k_dn), j).wait_send()))

    loop(1, 16, lambda o: wf_copy(o).wait_send())
    wf_sib(c).wait_send()

    def kv_sent(s):
        @pl.when(jnp.logical_and(z >= s - 1, z < ZN - 1))
        def _():
            up_copy(s, z).wait_send()

        @pl.when(jnp.logical_and(s < 8, jnp.logical_or(z + s <= 7, z + s >= ZN + 1)))
        def _():
            dn_copy(s, z).wait_send()

        @pl.when(z >= s)
        def _():
            sib_copy(2 * s, z, c).wait_send()

        @pl.when(jnp.logical_and(s < 8, z + s >= ZN))
        def _():
            sib_copy(2 * s + 1, z, c).wait_send()

    sib_copy(0, z, c).wait_send()
    loop(1, 9, kv_sent)
    for h in range(2):
        here = jnp.logical_and(is_self, x % 2 == h)

        @pl.when(jnp.logical_not(here))
        def _():
            dst = kvbuf.at[z, x // 2, rows, :]
            dest_sp = z * 4 + 2 * c + h
            copy_to(kvsend.at[h], dst, kv_s.at[h], kv_r.at[x % 2], dest_sp, dest_dp).wait_send()
            copy_to(qsend.at[h], qbuf.at[x % 2], q_s.at[h], q_r.at[x % 2], dest_sp, dest_dp).wait_send()
            copy_to(pstage.at[h], pbuf.at[x % 2], p_s.at[h], p_r.at[x % 2], dest_sp, dest_dp).wait_send()

    for r in range(2):
        loop(1, 32, lambda o, r=r: there(o, r).wait_send())
    keep_first.wait()
    keep_second.wait()
    for r in range(2):
        loop(1, 32, lambda o, r=r: back(o, r).wait_recv())
    mixed = dot(c_ref[...], retb[...].reshape(1024, 1024))
    out_ref[...] = (resid[...] + (mixed[0:TOK, :] + mixed[TOK : 2 * TOK, :])).astype(BF16)
    for r in range(2):
        loop(1, 32, lambda o, r=r: back(o, r).wait_send())


def body(
    hidden_in, queries, keys, values, q_gain, k_gain, out_weight, moe_gain,
    expert_ids, route_weights, gate_proj, up_proj, down_proj,
):
    sp = lax.axis_index("sp")
    positions = sp * TOK + jnp.arange(TOK, dtype=jnp.int32)
    expo = jnp.arange(64).astype(F32) * (-2.0 / 128)
    freq = jnp.power(jnp.float32(THETA), expo)
    angle = positions.astype(F32)[:, None] * freq[None, :]
    cosv = jnp.cos(angle)
    sinv = jnp.sin(angle)
    cos2 = jnp.concatenate([cosv, cosv], axis=-1)
    sin2 = jnp.concatenate([-sinv, sinv], axis=-1)
    vm = pl.BlockSpec(memory_space=pltpu.VMEM)
    hbm = pl.BlockSpec(memory_space=pltpu.HBM)
    dma = pltpu.SemaphoreType.DMA

    return pl.pallas_call(
        layer_kernel,
        out_shape=jax.ShapeDtypeStruct((TOK, 1024), BF16),
        in_specs=[hbm] * 15,
        out_specs=vm,
        scratch_shapes=[
            pltpu.VMEM((TOK, 2048), BF16),
            pltpu.VMEM((TOK, 256), BF16),
            pltpu.VMEM((TOK, 256), BF16),
            pltpu.VMEM((1, 128), F32),
            pltpu.VMEM((1, 128), F32),
            pltpu.VMEM((TOK, 128), F32),
            pltpu.VMEM((TOK, 128), F32),
            pltpu.VMEM((16, 2048), BF16),
            pltpu.VMEM((TOK, 1024), BF16),
            pltpu.VMEM((1, 1024), F32),
            pltpu.VMEM((8, TOK), jnp.int32),
            pltpu.VMEM((8, TOK), F32),
            pltpu.VMEM((64 * SLOT, TOK), BF16),
            pltpu.VMEM((2 * TOK, 64 * SLOT), BF16),
            dma((12,)),
            pltpu.VMEM((2, TOK, 1024), BF16),
            pltpu.VMEM((2, TOK, 256), BF16),
            pltpu.VMEM((2, TOK, 1024), BF16),
            pltpu.VMEM((1536, 128), BF16),
            pltpu.VMEM((ZN, 2, 192, 256), BF16),
            pltpu.VMEM((1536, 128), F32),
            pltpu.VMEM((1536, 128), F32),
            pltpu.VMEM((192, 1024), BF16),
            pltpu.VMEM((2, 16, 2048), BF16),
            pltpu.VMEM((2, 4, 2, 4, 16, 1024), BF16),
            pltpu.VMEM((2, TOK, 1024), BF16),
            pltpu.VMEM((2, TOK, 1024), BF16),
            pltpu.VMEM((TOK, 1024), F32),
            pltpu.VMEM((32, 2, SLOT, 1024), BF16),
            pltpu.VMEM((2, 32, SLOT, 1024), BF16),
            pltpu.VMEM((2, 32, SLOT, 1024), BF16),
            pltpu.VMEM((32, 2, SLOT, 1024), BF16),
            pltpu.VMEM((2, 1024, 384), BF16),
            pltpu.VMEM((2, 1024, 384), BF16),
            pltpu.VMEM((2, 384, 1024), BF16),
            dma((2,)), dma((2,)), dma((2,)), dma((2,)),
            dma((9,)), dma((9,)), dma((9,)), dma((9,)),
            dma((17,)), dma((17,)),
            dma((4,)), dma((2,)), dma((16,)), dma((16,)),
            dma((2,)), dma((2,)), dma((4,)),
            dma((NPIECE,)), dma((NPIECE,)), dma((NPIECE,)), dma((NPIECE,)),
            dma((4,)),
            dma((2, 32)), dma((2, 32)), dma((2, 32)), dma((2, 32)),
        ],
        compiler_params=pltpu.CompilerParams(
            collective_id=0, has_side_effects=True, vmem_limit_bytes=63 * 1024 * 1024
        ),
        name="layer",
    )(
        queries, keys, values, q_gain.reshape(1, 128), k_gain.reshape(1, 128), cos2, sin2, out_weight.T,
        hidden_in, moe_gain.reshape(1, 1024), expert_ids.T, route_weights.T, gate_proj[0], up_proj[0], down_proj[0],
    )


def solution(mesh):
    tok = P(("dp", "sp"), None)
    return jax.shard_map(
        body,
        mesh=mesh,
        in_specs=(
            tok, tok, tok, tok, P(), P(), P(None, "sp"), P(), tok, tok,
            P("sp", None, None), P("sp", None, None), P("sp", None, None),
        ),
        out_specs=tok,
        check_vma=False,
    )
```
